512 devices in a mesh: grp: 64 (over x_lo, z, core), head: 8 (over y, x_hi).
Axes of the slice: x: 4 (x_hi: 2, x_lo: 2; x = x_hi * 2 + x_lo), y: 4, z: 16, core: 2. Of those that a mesh axis runs over, the one named last changes fastest.
Arguments:
- resident_latent_cache: bfloat16 [256, 256, 576], P('grp'), may hold values from -6 to 6
- resident_len: int32 [64, 4], P('grp'), may hold values from 1 to 256, 640 in all within a row
- resident_query: bfloat16 [3, 256, 128, 576], P(None, 'grp', 'head'), may hold values from -49 to 49
- step_latent: bfloat16 [3, 256, 576], P(None, 'grp'), may hold values from -6 to 6
- prompt_cache: bfloat16 [256, 1024, 576], P('grp', 'head'), may hold values from -6 to 6
- prompt_query: bfloat16 [256, 128, 576], P('grp', 'head'), may hold values from -49 to 49
- prompt_len: int32 [64, 4], replicated, may hold values from 1 to 1024, 2560 in all within a row
- route_offset: int32 [64, 4, 1], replicated, may hold values from 0 to 3; in each aligned block of 4 rows (0 to 3, 4 to 7, ..., all dimensions but the last counted through in order) at most 2 rows name the same one
Outputs:
- resident_out: bfloat16 [3, 256, 128, 512], P(None, 'grp', 'head')
- first_out: bfloat16 [64, 8, 128, 512], P('grp', None, 'head')
- arrived_cache: bfloat16 [64, 8, 1024, 576], P('grp', None, 'head')
The draws below stay inside these ranges and needn't reach their ends.
Inputs may be any that keep to these rules, and one draw needn't show every extreme that they name: `resident_len`: in every group one sequence fills all 256 cache slots. `prompt_len`: in every prefill group one prompt fills all 1024 positions. `route_offset`: among the 4 prompts of one prefill group no value is named more than 2 times; in some prefill groups one value is named exactly 2 times, and every value is named by some prompt.
All inputs are finite; a program needn't handle non-finite values.
Results may differ from the reference program's by a relative error of at most 0.015.
Values may be sent and summed in bfloat16 or wider, within the bound.
A program may use at most 64 MiB of HBM per device.

```python
import math
import jax
import jax.numpy as jnp
import numpy as np
from jax import lax

HEADS = 128
LATENT_RANK = 512
LATENT_WIDTH = 576
SEQ_GRP = 4
RES_LEN = 256
STEPS = 3
PROMPT_MAX = 1024
PROMPT_GRP = 4
REACH = 4
CAPACITY = 2
ARRIVE = 8
SEQS = 256
PROMPTS = 256
N_GRP = 64


def anchor_rows(key, marker, count):
    key = jax.random.fold_in(key, marker)
    return jnp.clip(jax.random.normal(key, (count, LATENT_WIDTH), jnp.float32), -6.0, 6.0)


def cache_rows(key, anchor, count, length):
    values = jnp.clip(jax.random.normal(key, (count, length, LATENT_WIDTH), jnp.float32), -6.0, 6.0)
    return values.at[:, 0, :].set(anchor)


def draw_resident_latent_cache(key, part):
    anchor = anchor_rows(key, 1, SEQS)
    key = jax.random.fold_in(key, 3)
    base = cache_rows(key, anchor, SEQS, RES_LEN)
    return base.astype(jnp.bfloat16)


def draw_resident_query(key, part):
    key = jax.random.fold_in(key, 4)
    draws = jnp.clip(jax.random.normal(key, (STEPS, SEQS, HEADS, LATENT_WIDTH), jnp.float32), -6.0, 6.0)
    return draws.astype(jnp.bfloat16)


def draw_prompt_cache(key, part):
    anchor = anchor_rows(key, 2, PROMPTS)
    key = jax.random.fold_in(key, 6)
    base = cache_rows(key, anchor, PROMPTS, PROMPT_MAX)
    return base.astype(jnp.bfloat16)


def draw_prompt_query(key, part):
    key = jax.random.fold_in(key, 7)
    draws = jnp.clip(jax.random.normal(key, (PROMPTS, HEADS, LATENT_WIDTH), jnp.float32), -6.0, 6.0)
    return draws.astype(jnp.bfloat16)


def shard_levels(own_key, extent, cuts, smallest, high):
    gain = 1.0
    for dim, shards_of in cuts:
        steps = jax.random.uniform(jax.random.fold_in(jax.random.fold_in(own_key, 6), dim), (shards_of,), jnp.float32, smallest / len(cuts), high / len(cuts))
        gain = gain * jnp.repeat(jnp.exp(steps), extent[dim] // shards_of).reshape((-1,) + (1,) * (len(extent) - 1 - dim))
    return gain


def profile(count, total, bound, lean):
    portions = [(1 << 20) // math.isqrt(rank ** lean) + 1 for rank in range(2, count + 1)]
    surplus, given = total - bound - (count - 1), [1] * (count - 1)
    while surplus > 0:
        movable = [i for i in range(count - 1) if given[i] < bound]
        mass, left = sum([portions[i] for i in movable]), surplus
        for i in movable:
            addition = min(bound - given[i], max(1, left * portions[i] // mass), surplus)
            given[i] = given[i] + addition
            surplus = surplus - addition
    return np.array([bound] + given)


def uneven(rng, count, total, most, lean):
    if count == 2:
        one = jax.random.randint(rng, (), max(1, total - most), min(most, total - 1) + 1)
        return jnp.stack([one, total - one])
    tallies = jnp.asarray(profile(count, total, most, lean), jnp.int32)
    twos = (count - 1) // 2
    source_of, receiver = tallies[1:1 + 2 * twos:2], tallies[2:2 + 2 * twos:2]
    room = jnp.minimum(source_of - 1, most - receiver)
    passed = jax.random.randint(jax.random.fold_in(rng, 1), (twos,), 0, 1 << 20) % (room + 1)
    tallies = tallies.at[1:1 + 2 * twos:2].set(source_of - passed).at[2:2 + 2 * twos:2].set(receiver + passed)
    return tallies[jax.random.permutation(jax.random.fold_in(rng, 2), count)]


def shared_out(key, own, number, rows, number_of, top, most, lean):
    sequence = jax.random.permutation(key, number_of)
    crowded, ordinary = shares(number_of, rows * top, most, lean, True), shares(number_of, rows * top, most, lean, False)
    places = jnp.arange(number_of)

    def named(sizes, rotation):
        used = int((sizes > 0).sum())
        fixed = max(1, used // 4)
        moved = fixed + (places - fixed + rotation * (used - fixed)) % max(1, number_of - fixed)
        return jnp.zeros((number_of,), jnp.int32).at[sequence[jnp.where(places < fixed, places, moved)]].set(jnp.asarray(sizes, jnp.int32))

    sizes = jnp.where(number % 4 == 0, named(crowded, number // 4), named(ordinary, number - number // 4 - 1))
    mixed = jax.random.permutation(jax.random.fold_in(own, 3), number_of)
    donor, sink = mixed[0:number_of // 2 * 2:2], mixed[1:number_of // 2 * 2:2]
    margin = jnp.minimum(sizes[donor] - 1, most - sizes[sink]) // 2
    margin = jnp.where((donor == sequence[0]) | (sink == sequence[0]) | (sizes[sink] == 0), 0, jnp.maximum(margin, 0))
    moved = jax.random.randint(jax.random.fold_in(own, 4), (number_of // 2,), 0, 1 << 20) % (margin + 1)
    sizes = sizes.at[donor].add(-moved).at[sink].add(moved)
    members = jnp.searchsorted(jnp.cumsum(sizes), jnp.arange(rows * top), side="right").astype(jnp.int32)
    grid = members.reshape(top, rows).T
    grid = grid[jax.random.permutation(jax.random.fold_in(own, 1), rows)]
    rotation = jax.random.randint(jax.random.fold_in(own, 2), (rows, 1), 0, top)
    return jnp.take_along_axis(grid, (jnp.arange(top)[None, :] + rotation) % top, axis=1)


def shares(count, total, reach, lean, full):
    loads = [(1 << 20) // math.isqrt(standing ** lean) + 1 for standing in range(1, count + 1)]
    largest = reach if full else min(reach, max(-(-total // count), total * loads[0] // sum(loads)))
    least = 1 if total - largest >= count - 1 else 0
    counts, spare = [largest] + [least] * (count - 1), total - largest - least * (count - 1)
    while spare > 0:
        movable = [i for i in range(1, count) if counts[i] < largest] or [i for i in range(1, count) if counts[i] < reach]
        mass, left = sum([loads[i] for i in movable]), spare
        for i in movable:
            addition = min(reach - counts[i], max(1, left * loads[i] // mass), spare)
            counts[i] = counts[i] + addition
            spare = spare - addition
    return np.array(counts)


def gaussian(rng, shape, deviation, limit, shards=(), held_as=jnp.bfloat16):
    entries = jax.random.normal(rng, shape, jnp.float32) * deviation
    if len(shards) > 0:
        entries = shard_levels(rng, shape, shards, -0.22, 0.18) * entries
    return jnp.clip(entries, min=-limit, max=limit).astype(held_as)


def setup_inputs(seed: int = 0) -> dict:
    arg_keys = jax.random.split(jax.random.key(seed), 9)
    resident_latent_cache = draw_resident_latent_cache(jax.random.fold_in(arg_keys[8], 71), 0)
    resident_len = jax.vmap(lambda own: uneven(own, SEQ_GRP, (SEQ_GRP + 1) * RES_LEN // 2, RES_LEN, 2))(jax.random.split(arg_keys[1], N_GRP)).reshape((N_GRP, SEQ_GRP)).astype(jnp.int32)
    resident_query = draw_resident_query(jax.random.fold_in(arg_keys[8], 71), 0)
    step_latent = gaussian(arg_keys[3], (STEPS, SEQS, LATENT_WIDTH), 1.0, 6.0, ((1, 64),))
    prompt_cache = draw_prompt_cache(jax.random.fold_in(arg_keys[8], 71), 0)
    prompt_query = draw_prompt_query(jax.random.fold_in(arg_keys[8], 71), 0)
    prompt_len = jax.vmap(lambda own: uneven(own, PROMPT_GRP, (PROMPT_GRP + 1) * PROMPT_MAX // 2, PROMPT_MAX, 2))(jax.random.split(arg_keys[6], N_GRP)).reshape((N_GRP, PROMPT_GRP)).astype(jnp.int32)
    route_offset_keys = jax.random.split(jax.random.fold_in(arg_keys[7], 1), N_GRP * PROMPT_GRP // PROMPT_GRP)
    route_offset_turns = jax.random.permutation(jax.random.fold_in(arg_keys[7], 3), N_GRP * PROMPT_GRP // PROMPT_GRP)
    route_offset = jax.vmap(lambda own, number: shared_out(jax.random.fold_in(arg_keys[7], 2), own, number, PROMPT_GRP, REACH, 1, CAPACITY, 2))(route_offset_keys, route_offset_turns).reshape((N_GRP, PROMPT_GRP, 1))
    return dict(resident_latent_cache=resident_latent_cache, resident_len=resident_len, resident_query=resident_query, step_latent=step_latent, prompt_cache=prompt_cache, prompt_query=prompt_query, prompt_len=prompt_len, route_offset=route_offset)


score_scale = 192.0 ** -0.5
low_value = -1e30


def weights_bfloat(attention_weights):
    return lax.optimization_barrier(attention_weights.astype(jnp.bfloat16)).astype(jnp.float32)


def resident_part(resident_latent_cache, resident_len, resident_query, step_latent):
    queries = resident_query.astype(jnp.float32)
    resident_block = resident_latent_cache.astype(jnp.float32)
    fresh_rows = step_latent.astype(jnp.float32)
    lengths = resident_len.reshape(SEQS)
    old_scores = jnp.einsum("tshk,sjk->tshj", queries, resident_block) * score_scale
    new_scores = jnp.einsum("tshk,usk->tshu", queries, fresh_rows) * score_scale
    places = jnp.arange(RES_LEN, dtype=jnp.int32)
    old_live = (places[None, :] < lengths[:, None])[None, :, None, :]
    step_ids = jnp.arange(STEPS, dtype=jnp.int32)
    new_live = (step_ids[None, :] <= step_ids[:, None])[:, None, None, :]
    old_scores = jnp.where(old_live, old_scores, low_value)
    new_scores = jnp.where(new_live, new_scores, low_value)
    row_max = jnp.maximum(jnp.max(old_scores, -1), jnp.max(new_scores, -1))[..., None]
    prior_exponent = jnp.where(old_live, jnp.exp(old_scores - row_max), 0.0)
    fresh_exponent = jnp.where(new_live, jnp.exp(new_scores - row_max), 0.0)
    softmax_total = jnp.sum(prior_exponent, -1) + jnp.sum(fresh_exponent, -1)
    blended_output = jnp.einsum("blan,lnw->blaw", weights_bfloat(prior_exponent), resident_block[:, :, :LATENT_RANK])
    blended_output = blended_output + jnp.einsum("izpl,lzo->izpo", weights_bfloat(fresh_exponent), fresh_rows[:, :, :LATENT_RANK])
    return (blended_output / softmax_total[..., None]).astype(jnp.bfloat16)


def reference(resident_latent_cache, resident_len, resident_query, step_latent, prompt_cache, prompt_query, prompt_len, route_offset):
    resident_out = resident_part(resident_latent_cache, resident_len, resident_query, step_latent)
    prompt_off = route_offset.reshape(N_GRP, PROMPT_GRP)
    same_off = prompt_off[:, :, None] == prompt_off[:, None, :]
    earlier = jnp.arange(PROMPT_GRP, dtype=jnp.int32)[None, :] < jnp.arange(PROMPT_GRP, dtype=jnp.int32)[:, None]
    slot_rank = jnp.sum((same_off & earlier[None]).astype(jnp.int32), -1)
    flat_off = prompt_off.reshape(PROMPTS)
    flat_rank = slot_rank.reshape(PROMPTS)
    flat_len = prompt_len.reshape(PROMPTS)
    prompt_ids = jnp.arange(PROMPTS, dtype=jnp.int32)
    prompt_group = prompt_ids // PROMPT_GRP
    slot_ids = jnp.arange(ARRIVE, dtype=jnp.int32)
    slot_reach = slot_ids // CAPACITY
    slot_place = slot_ids % CAPACITY
    places = jnp.arange(PROMPT_MAX, dtype=jnp.int32)

    def one_dest(dest_group):
        sources = (dest_group - 1 - slot_reach) % N_GRP
        matched = (prompt_group[None, :] == sources[:, None]) & (flat_off[None, :] == slot_reach[:, None]) & (flat_rank[None, :] == slot_place[:, None])
        is_filled = jnp.any(matched, -1)
        source_index = jnp.sum(jnp.where(matched, prompt_ids[None, :], 0), -1).astype(jnp.int32)
        slot_len = jnp.sum(jnp.where(matched, flat_len[None, :], 0), -1).astype(jnp.int32)
        token_live = places[None, :] < slot_len[:, None]
        key_latent_rows = jnp.where(token_live[:, :, None], prompt_cache[source_index], jnp.zeros((), jnp.bfloat16))
        query_rows = jnp.where(is_filled[:, None, None], prompt_query[source_index], jnp.zeros((), jnp.bfloat16))
        expanded_keys = key_latent_rows.astype(jnp.float32)
        scores = jnp.einsum("shk,sjk->shj", query_rows.astype(jnp.float32), expanded_keys) * score_scale
        is_live = token_live[:, None, :]
        scores = jnp.where(is_live, scores, low_value)
        row_max = jnp.max(scores, -1, keepdims=True)
        attention_weights = jnp.where(is_live, jnp.exp(scores - row_max), 0.0)
        softmax_total = jnp.sum(attention_weights, -1, keepdims=True)
        blended_output = jnp.einsum("pei,pio->peo", weights_bfloat(attention_weights), expanded_keys[:, :, :LATENT_RANK])
        first_rows = (blended_output / jnp.maximum(softmax_total, 1.0)).astype(jnp.bfloat16)
        return first_rows, key_latent_rows

    first_out, arrived_cache = lax.map(one_dest, jnp.arange(N_GRP, dtype=jnp.int32))
    return resident_out, first_out, arrived_cache
```

```python
import functools

import jax
import jax.numpy as jnp
from jax import lax
from jax.experimental import pallas as pl
from jax.experimental.pallas import tpu as pltpu
from jax.sharding import PartitionSpec as P

LATENT_RANK = 512
REACH = 4
CAPACITY = 2
MESH = pl.DeviceIdType.MESH
SCALE = 192.0 ** (-0.5)
LOW = -1e30
NEW_ROWS = 16

NN = (((1,), (0,)), ((), ()))
NT = (((1,), (1,)), ((), ()))


def matmul(a, b, dims):
    return lax.dot_general(a, b, dims, preferred_element_type=jnp.float32)


def kernel(
    groups, lanes,
    plen, roff, rlen, sl, rct, rq, pct, pq,
    ro, fo, ac,
    rctv, rqv, pctv, qall, newk, newkf, obuf, rbuf, stat, rstat, rows, frows, fsend, rov,
    load_sem, out_sem, q_send, q_recv, o_send, o_recv, s_send, s_recv, c_send, c_recv, f_send, f_recv,
):
    me = lax.axis_index("grp")
    lane = lax.axis_index("head")
    prompts, width, part = pct.shape
    seqs = rct.shape[0]
    res_len = rct.shape[2]
    steps, _, heads, _ = rq.shape

    loads = [
        pltpu.make_async_copy(src, dst, load_sem.at[i])
        for i, (src, dst) in enumerate(((pct, pctv), (pq, qall.at[0]), (rct, rctv), (rq, rqv)))
    ]
    for copy in loads:
        copy.start()

    def on_lane(k):
        return (me, lax.rem(lane + k, lanes))

    def on_group(k):
        return (lax.rem(me + k + groups, groups), lane)

    barrier = pltpu.get_barrier_semaphore()
    for k in range(1, lanes):
        pl.semaphore_signal(barrier, inc=1, device_id=on_lane(k), device_id_type=MESH)
    for k in range(1, REACH + 1):
        pl.semaphore_signal(barrier, inc=1, device_id=on_group(k), device_id_type=MESH)
        pl.semaphore_signal(barrier, inc=1, device_id=on_group(-k), device_id_type=MESH)
    pl.semaphore_wait(barrier, lanes - 1 + 2 * REACH)

    def remote(src, dst, send, recv, to):
        return pltpu.make_async_remote_copy(
            src_ref=src, dst_ref=dst, send_sem=send, recv_sem=recv, device_id=to, device_id_type=MESH
        )

    q_copies = [
        remote(pq, qall.at[k], q_send.at[k], q_recv.at[k], on_lane(k)) for k in range(1, lanes)
    ]
    for copy in q_copies:
        copy.start()

    offs = [roff[i, me] for i in range(prompts)]
    lens = [plen[i, me] - lane * part for i in range(prompts)]
    ranks = []
    for i in range(prompts):
        rank = jnp.int32(0)
        for i2 in range(i):
            rank = rank + jnp.where(offs[i2] == offs[i], 1, 0)
        ranks.append(rank)

    def pick(distance, place):
        index, length, filled = jnp.int32(0), jnp.int32(0), jnp.int32(0)
        for i in range(prompts):
            hit = jnp.logical_and(offs[i] == distance, ranks[i] == place)
            index = jnp.where(hit, i, index)
            length = jnp.where(hit, lens[i], length)
            filled = jnp.where(hit, 1, filled)
        return index, length, filled

    slots = [[pick(d, r) for r in range(CAPACITY)] for d in range(REACH)]

    loads[0].wait()
    places = lax.broadcasted_iota(jnp.int32, (width, part), 1)
    c_copies = []
    for d in range(REACH):
        for r in range(CAPACITY):
            index, length, _ = slots[d][r]
            block = pctv[index]
            rows[d, r] = jnp.where(places < length, block, jnp.zeros_like(block))
        copy = remote(
            rows.at[d], ac.at[pl.ds(d * CAPACITY, CAPACITY)], c_send.at[d], c_recv.at[d], on_group(d + 1)
        )
        copy.start()
        c_copies.append(copy)

    newkf[...] = jnp.zeros_like(newkf)
    for u in range(steps):
        step_rows = sl[u].astype(jnp.float32)
        for s in range(seqs):
            newkf[pl.ds(s * NEW_ROWS + u, 1), :] = step_rows[s:s + 1, :]
    newk[...] = newkf[...].astype(jnp.bfloat16)
    loads[2].wait()
    loads[3].wait()

    def resident(s):
        count = steps * heads
        query = rqv[:, s].reshape(count, width)
        fresh = newk.shape[0]
        old = matmul(query, rctv[s], NN) * SCALE
        new = matmul(query, newk[...], NT) * SCALE
        old_live = lax.broadcasted_iota(jnp.int32, (count, res_len), 1) < rlen[0, s]
        step = lax.broadcasted_iota(jnp.int32, (count, fresh), 0) // heads
        token = lax.broadcasted_iota(jnp.int32, (count, fresh), 1) - s * NEW_ROWS
        new_live = jnp.logical_and(token >= 0, token <= step)
        old = jnp.where(old_live, old, LOW)
        new = jnp.where(new_live, new, LOW)
        top = jnp.maximum(jnp.max(old, 1, keepdims=True), jnp.max(new, 1, keepdims=True))
        old = jnp.where(old_live, jnp.exp(old - top), 0.0)
        new = jnp.where(new_live, jnp.exp(new - top), 0.0)
        total = jnp.sum(old, 1, keepdims=True) + jnp.sum(new, 1, keepdims=True)
        mixed = matmul(old.astype(jnp.bfloat16), rctv[s, :LATENT_RANK, :], NT)
        mixed = mixed + matmul(new.astype(jnp.bfloat16), newk[:, :LATENT_RANK], NN)
        rov[:, s] = (mixed / total).astype(jnp.bfloat16).reshape(steps, heads, LATENT_RANK)

    for s in range(seqs // 2):
        resident(s)

    loads[1].wait()
    for copy in q_copies:
        copy.wait_recv()
    all_heads = lanes * heads
    column = lax.broadcasted_iota(jnp.int32, (all_heads, 128), 1)
    stats = jnp.zeros((all_heads, 128), jnp.float32)
    spots = lax.broadcasted_iota(jnp.int32, (all_heads, part), 1)
    for p in range(prompts):
        query = qall[:, p].reshape(all_heads, width)
        live = spots < lens[p]
        scores = jnp.where(live, matmul(query, pctv[p], NN) * SCALE, LOW)
        top = jnp.max(scores, 1, keepdims=True)
        weights = jnp.where(live, jnp.exp(scores - top), 0.0)
        total = jnp.sum(weights, 1, keepdims=True)
        mixed = matmul(weights.astype(jnp.bfloat16), pctv[p, :LATENT_RANK, :], NT)
        obuf[:, p] = mixed.astype(jnp.bfloat16).reshape(lanes, heads, LATENT_RANK)
        stats = jnp.where(column == 2 * p, top, stats)
        stats = jnp.where(column == 2 * p + 1, total, stats)
    stat[...] = stats.reshape(lanes, heads, 128)

    o_copies = []
    for k in range(1, lanes):
        to = on_lane(lanes - k)
        o_copies.append(remote(obuf.at[k], rbuf.at[k], o_send.at[k], o_recv.at[k], to))
        o_copies.append(remote(stat.at[k], rstat.at[k], s_send.at[k], s_recv.at[k], to))
    for copy in o_copies:
        copy.start()

    for s in range(seqs // 2, seqs):
        resident(s)
    keep = pltpu.make_async_copy(rov, ro, out_sem)
    keep.start()

    for copy in o_copies:
        copy.wait_recv()
    for p in range(prompts):
        tops = [(stat if k == 0 else rstat)[k, :, 2 * p:2 * p + 1] for k in range(lanes)]
        sums = [(stat if k == 0 else rstat)[k, :, 2 * p + 1:2 * p + 2] for k in range(lanes)]
        top = functools.reduce(jnp.maximum, tops)
        total = jnp.zeros_like(top)
        mixed = jnp.zeros((heads, LATENT_RANK), jnp.float32)
        for k in range(lanes):
            factor = jnp.exp(tops[k] - top)
            total = total + factor * sums[k]
            mixed = mixed + factor * (obuf if k == 0 else rbuf)[k, p].astype(jnp.float32)
        frows[p] = (mixed / jnp.maximum(total, 1.0)).astype(jnp.bfloat16)

    spread = lax.broadcasted_iota(jnp.int32, (heads, LATENT_RANK), 0)
    f_copies = []
    for d in range(REACH):
        for r in range(CAPACITY):
            index, _, filled = slots[d][r]
            block = frows[index]
            fsend[d, r] = jnp.where(spread < filled * heads, block, jnp.zeros_like(block))
        copy = remote(
            fsend.at[d], fo.at[pl.ds(d * CAPACITY, CAPACITY)], f_send.at[d], f_recv.at[d], on_group(d + 1)
        )
        copy.start()
        f_copies.append(copy)

    keep.wait()
    for copy in q_copies + o_copies:
        copy.wait_send()
    for copy in c_copies + f_copies:
        copy.wait_send()
        copy.wait_recv()


def call(mesh_shape, plen, roff, rlen, sl, rct, rq, pct, pq):
    groups, lanes = mesh_shape
    prompts, width, part = pct.shape
    steps, seqs, heads, _ = rq.shape
    slots = REACH * CAPACITY
    bf, f32 = jnp.bfloat16, jnp.float32
    dma = pltpu.SemaphoreType.DMA
    anywhere = pl.BlockSpec(memory_space=pl.ANY)
    scalars = pl.BlockSpec(memory_space=pltpu.SMEM)
    return pl.pallas_call(
        functools.partial(kernel, groups, lanes),
        out_shape=(
            jax.ShapeDtypeStruct((steps, seqs, heads, LATENT_RANK), bf),
            jax.ShapeDtypeStruct((slots, heads, LATENT_RANK), bf),
            jax.ShapeDtypeStruct((slots, width, part), bf),
        ),
        in_specs=[scalars] * 3 + [pl.BlockSpec(memory_space=pltpu.VMEM)] + [anywhere] * 4,
        out_specs=(anywhere,) * 3,
        scratch_shapes=[
            pltpu.VMEM(rct.shape, bf),
            pltpu.VMEM(rq.shape, bf),
            pltpu.VMEM(pct.shape, bf),
            pltpu.VMEM((lanes,) + pq.shape, bf),
            pltpu.VMEM((128, width), bf),
            pltpu.VMEM((128, width), f32),
            pltpu.VMEM((lanes, prompts, heads, LATENT_RANK), bf),
            pltpu.VMEM((lanes, prompts, heads, LATENT_RANK), bf),
            pltpu.VMEM((lanes, heads, 128), f32),
            pltpu.VMEM((lanes, heads, 128), f32),
            pltpu.VMEM((REACH, CAPACITY, width, part), bf),
            pltpu.VMEM((prompts, heads, LATENT_RANK), bf),
            pltpu.VMEM((REACH, CAPACITY, heads, LATENT_RANK), bf),
            pltpu.VMEM((steps, seqs, heads, LATENT_RANK), bf),
            dma((4,)),
            dma,
            dma((lanes,)), dma((lanes,)),
            dma((lanes,)), dma((lanes,)),
            dma((lanes,)), dma((lanes,)),
            dma((REACH,)), dma((REACH,)),
            dma((REACH,)), dma((REACH,)),
        ],
        compiler_params=pltpu.CompilerParams(
            collective_id=0, has_side_effects=True, vmem_limit_bytes=40 * 1024 * 1024
        ),
        name="decode_and_migrate",
    )(plen, roff, rlen, sl, rct, rq, pct, pq)


def solution(mesh):
    mesh_shape = (mesh.shape["grp"], mesh.shape["head"])

    def body(
        resident_latent_cache, resident_len, resident_query, step_latent,
        prompt_cache, prompt_query, prompt_len, route_offset,
    ):
        ro, fo, ac = call(
            mesh_shape,
            prompt_len.T,
            route_offset[:, :, 0].T,
            resident_len,
            step_latent,
            jnp.swapaxes(resident_latent_cache, 1, 2),
            resident_query,
            jnp.swapaxes(prompt_cache, 1, 2),
            prompt_query,
        )
        return ro, fo[None], jnp.swapaxes(ac, 1, 2)[None]

    in_specs = (
        P("grp", None, None),
        P("grp", None),
        P(None, "grp", "head", None),
        P(None, "grp", None),
        P("grp", "head", None),
        P("grp", "head", None),
        P(),
        P(),
    )
    out_specs = (
        P(None, "grp", "head", None),
        P("grp", None, "head", None),
        P("grp", None, "head", None),
    )
    return jax.shard_map(body, mesh=mesh, in_specs=in_specs, out_specs=out_specs, check_vma=False)
```

```python
import functools

import jax
import jax.numpy as jnp
from jax import lax
from jax.experimental import pallas as pl
from jax.experimental.pallas import tpu as pltpu
from jax.sharding import PartitionSpec as P

LATENT_RANK = 512
REACH = 4
CAPACITY = 2
MESH = pl.DeviceIdType.MESH
SCALE = 192.0 ** (-0.5)
LOW = -1e30
NEW_ROWS = 16

FAR = 2
PIECES = 4

NN = (((1,), (0,)), ((), ()))
NT = (((1,), (1,)), ((), ()))


def matmul(a, b, dims):
    return lax.dot_general(a, b, dims, preferred_element_type=jnp.float32)


def kernel(
    groups, lanes,
    plen, roff, rlen, sl, rct, rq, pct, pq,
    ro, fo, ac,
    rctv, rqv, pctv, slv, qall, newk, newkf, obuf, rbuf, stat, rstat, xbuf, xrec, xstat, xrstat, near, picked, frows, fsend, rov,
    load_sem, out_sem, q_send, q_recv, o_send, o_recv, s_send, s_recv, x_send, x_recv,
    w_send, w_recv, n_send, n_recv, p_send, p_recv, keep_sem, f_send, f_recv,
    *wholes,
):
    me = lax.axis_index("grp")
    lane = lax.axis_index("head")
    core = lax.rem(me, 2)
    prompts, width, part = pct.shape
    seqs = rct.shape[0]
    res_len = rct.shape[2]
    steps, _, heads, _ = rq.shape
    line = lanes // FAR
    piece = width // PIECES

    loads = [
        pltpu.make_async_copy(src, dst, load_sem.at[i])
        for i, (src, dst) in enumerate(((pct, pctv), (pq, qall.at[0]), (rct, rctv), (rq, rqv), (sl, slv)))
    ]
    for copy in loads:
        copy.start()

    y, x = lane // FAR, lax.rem(lane, FAR)

    def on_lane(j, k):
        return (me, lax.rem(y + k, line) * FAR + lax.rem(x + j, FAR))

    def on_group(k):
        return (lax.rem(me + k + groups, groups), lane)

    others = [(j, k) for j in range(FAR - 1, -1, -1) for k in range(line) if j or k]
    barrier = pltpu.get_barrier_semaphore()
    for k in range(1, REACH + 1):
        pl.semaphore_signal(barrier, inc=1, device_id=on_group(-k), device_id_type=MESH)
    for j, k in others:
        pl.semaphore_signal(barrier, inc=1, device_id=on_lane(j, k), device_id_type=MESH)

    @pl.when(core == 0)
    def _():
        pl.semaphore_signal(barrier, inc=1, device_id=on_group(1), device_id_type=MESH)

    pl.semaphore_wait(barrier, lanes - 1 + REACH + core)

    def remote(src, dst, send, recv, to):
        return pltpu.make_async_remote_copy(
            src_ref=src, dst_ref=dst, send_sem=send, recv_sem=recv, device_id=to, device_id_type=MESH
        )

    q_copies = {
        (j, k): remote(pq, qall.at[j * line + k], q_send.at[j, k], q_recv.at[j, k], on_lane(j, k))
        for j, k in others
    }
    for copy in q_copies.values():
        copy.start()

    def latent(i):
        return pl.ds(i * piece, piece)

    w_copies = [
        remote(pct.at[:, latent(i)], wholes[i], w_send.at[i], w_recv.at[i], on_group(2))
        for i in range(PIECES)
    ]
    for copy in w_copies:
        copy.start()

    def places_of(group):
        offs = [roff[i, group] for i in range(prompts)]
        lens = [plen[i, group] - lane * part for i in range(prompts)]
        ranks = []
        for i in range(prompts):
            rank = jnp.int32(0)
            for i2 in range(i):
                rank = rank + jnp.where(offs[i2] == offs[i], 1, 0)
            ranks.append(rank)

        def pick(distance, place):
            index, length, filled = jnp.int32(0), jnp.int32(0), jnp.int32(0)
            for i in range(prompts):
                hit = jnp.logical_and(offs[i] == distance, ranks[i] == place)
                index = jnp.where(hit, i, index)
                length = jnp.where(hit, lens[i], length)
                filled = jnp.where(hit, 1, filled)
            return index, length, filled

        return lens, [[pick(d, r) for r in range(CAPACITY)] for d in range(REACH)]

    lens, slots = places_of(me)
    _, passing = places_of(lax.rem(me + groups - 2, groups))

    spots = lax.broadcasted_iota(jnp.int32, (piece, part), 1)

    def masked(ref, rows, slot):
        index, length, _ = slot
        block = ref[index, rows, :]
        return jnp.where(spots < length, block, jnp.zeros_like(block))

    n_copies = [
        remote(
            near.at[:, latent(i)], ac.at[pl.ds(0, CAPACITY), latent(i)],
            n_send.at[i], n_recv.at[i], on_group(1 - 2 * core),
        )
        for i in range(PIECES)
    ]
    loads[0].wait()

    @pl.when(core == 0)
    def _():
        for i in range(PIECES):
            for r in range(CAPACITY):
                near[r, latent(i), :] = masked(pctv, latent(i), slots[0][r])
            n_copies[i].start()

    p_copies, keeps = [], []
    for i in range(PIECES):
        for d in range(1, REACH):
            src, dst = picked.at[d - 1, :, latent(i)], ac.at[pl.ds(d * CAPACITY, CAPACITY), latent(i)]
            if d == 1:
                keeps.append(pltpu.make_async_copy(src, dst, keep_sem.at[i]))
            else:
                p_copies.append(remote(src, dst, p_send.at[i, d], p_recv.at[i, d], on_group(d - 1)))

    def pass_on(i):
        w_copies[i].wait_recv()
        for d in range(REACH - 1, 0, -1):
            for r in range(CAPACITY):
                picked[d - 1, r, latent(i), :] = masked(wholes[i], slice(None), passing[d][r])
            if d == 1:
                keeps[i].start()
            else:
                p_copies[i * (REACH - 2) + d - 2].start()

        @pl.when(core == 1)
        def _():
            for r in range(CAPACITY):
                near[r, latent(i), :] = masked(wholes[i], slice(None), passing[0][r])
            n_copies[i].start()

    loads[4].wait()
    newkf[...] = jnp.zeros_like(newkf)
    for u in range(steps):
        step_rows = slv[u].astype(jnp.float32)
        for s in range(seqs):
            newkf[pl.ds(s * NEW_ROWS + u, 1), :] = step_rows[s:s + 1, :]
    newk[...] = newkf[...].astype(jnp.bfloat16)
    loads[2].wait()
    loads[3].wait()

    def resident(s):
        count = steps * heads
        query = rqv[:, s].reshape(count, width)
        fresh = newk.shape[0]
        old = matmul(query, rctv[s], NN) * SCALE
        new = matmul(query, newk[...], NT) * SCALE
        old_live = lax.broadcasted_iota(jnp.int32, (count, res_len), 1) < rlen[0, s]
        step = lax.broadcasted_iota(jnp.int32, (count, fresh), 0) // heads
        token = lax.broadcasted_iota(jnp.int32, (count, fresh), 1) - s * NEW_ROWS
        new_live = jnp.logical_and(token >= 0, token <= step)
        old = jnp.where(old_live, old, LOW)
        new = jnp.where(new_live, new, LOW)
        top = jnp.maximum(jnp.max(old, 1, keepdims=True), jnp.max(new, 1, keepdims=True))
        old = jnp.where(old_live, jnp.exp(old - top), 0.0)
        new = jnp.where(new_live, jnp.exp(new - top), 0.0)
        total = jnp.sum(old, 1, keepdims=True) + jnp.sum(new, 1, keepdims=True)
        mixed = matmul(old.astype(jnp.bfloat16), rctv[s, :LATENT_RANK, :], NT)
        mixed = mixed + matmul(new.astype(jnp.bfloat16), newk[:, :LATENT_RANK], NN)
        rov[:, s] = (mixed / total).astype(jnp.bfloat16).reshape(steps, heads, LATENT_RANK)

    for s in range(seqs // 2):
        resident(s)

    side = line * heads
    column = lax.broadcasted_iota(jnp.int32, (side, 128), 1)
    position = lax.broadcasted_iota(jnp.int32, (side, part), 1)
    o_copies = {}

    def attend(j):
        stats = jnp.zeros((side, 128), jnp.float32)
        for p in range(prompts):
            query = qall[pl.ds(j * line, line), p].reshape(side, width)
            live = position < lens[p]
            scores = jnp.where(live, matmul(query, pctv[p], NN) * SCALE, LOW)
            top = jnp.max(scores, 1, keepdims=True)
            weights = jnp.where(live, jnp.exp(scores - top), 0.0)
            total = jnp.sum(weights, 1, keepdims=True)
            mixed = matmul(weights.astype(jnp.bfloat16), pctv[p, :LATENT_RANK, :], NT)
            obuf[pl.ds(j * line, line), p] = mixed.astype(jnp.bfloat16).reshape(line, heads, LATENT_RANK)
            stats = jnp.where(column == 2 * p, top, stats)
            stats = jnp.where(column == 2 * p + 1, total, stats)
        stat[pl.ds(j * line, line)] = stats.reshape(line, heads, 128)
        o_copies[j] = []
        for k in range(1, line):
            slot, to = j * line + k, on_lane(0, line - k)
            o_copies[j].append(remote(obuf.at[slot], rbuf.at[slot], o_send.at[slot], o_recv.at[slot], to))
            o_copies[j].append(remote(stat.at[slot], rstat.at[slot], s_send.at[slot], s_recv.at[slot], to))
        for copy in o_copies[j]:
            copy.start()

    def merged(p, parts):
        tops = [where[:, 2 * p:2 * p + 1] for where, _ in parts]
        sums = [where[:, 2 * p + 1:2 * p + 2] for where, _ in parts]
        top = functools.reduce(jnp.maximum, tops)
        total = jnp.zeros_like(top)
        mixed = jnp.zeros((heads, LATENT_RANK), jnp.float32)
        for own_top, own_sum, (_, values) in zip(tops, sums, parts):
            factor = jnp.exp(own_top - top)
            total = total + factor * own_sum
            mixed = mixed + factor * values[p].astype(jnp.float32)
        return top, total, mixed

    def parts_of(j):
        slots_of = [j * line + k for k in range(line)]
        return [
            ((stat if k == 0 else rstat).at[slot], (obuf if k == 0 else rbuf).at[slot])
            for k, slot in enumerate(slots_of)
        ]

    for j, k in others:
        if j == 1:
            q_copies[j, k].wait_recv()
    attend(1)
    loads[1].wait()
    for j, k in others:
        if j == 0:
            q_copies[j, k].wait_recv()
    attend(0)

    for copy in o_copies[1]:
        copy.wait_recv()
    crossing = jnp.zeros((heads, 128), jnp.float32)
    lanes_of = lax.broadcasted_iota(jnp.int32, (heads, 128), 1)
    for p in range(prompts):
        top, total, mixed = merged(p, parts_of(1))
        xbuf[p] = mixed.astype(jnp.bfloat16)
        crossing = jnp.where(lanes_of == 2 * p, top, crossing)
        crossing = jnp.where(lanes_of == 2 * p + 1, total, crossing)
    xstat[...] = crossing
    x_copies = [
        remote(xbuf, xrec, x_send.at[0], x_recv.at[0], on_lane(1, 0)),
        remote(xstat, xrstat, x_send.at[1], x_recv.at[1], on_lane(1, 0)),
    ]
    for copy in x_copies:
        copy.start()

    for i in range(PIECES):
        pass_on(i)
        if i >= PIECES - seqs // 2:
            resident(i - PIECES + seqs)
    done = pltpu.make_async_copy(rov, ro, out_sem)
    done.start()

    for copy in o_copies[0] + x_copies:
        copy.wait_recv()
    for p in range(prompts):
        _, total, mixed = merged(p, parts_of(0) + [(xrstat, xrec)])
        frows[p] = (mixed / jnp.maximum(total, 1.0)).astype(jnp.bfloat16)

    spread = lax.broadcasted_iota(jnp.int32, (heads, LATENT_RANK), 0)
    f_copies = []
    for d in range(REACH - 1, -1, -1):
        for r in range(CAPACITY):
            index, _, filled = slots[d][r]
            block = frows[index]
            fsend[d, r] = jnp.where(spread < filled * heads, block, jnp.zeros_like(block))
        copy = remote(
            fsend.at[d], fo.at[pl.ds(d * CAPACITY, CAPACITY)], f_send.at[d], f_recv.at[d], on_group(d + 1)
        )
        copy.start()
        f_copies.append(copy)

    for copy in [done] + keeps:
        copy.wait()
    for copies in (q_copies.values(), o_copies[0], o_copies[1], x_copies, w_copies):
        for copy in copies:
            copy.wait_send()
    for copies in (n_copies, p_copies, f_copies):
        for copy in copies:
            copy.wait_send()
            copy.wait_recv()


def call(mesh_shape, plen, roff, rlen, sl, rct, rq, pct, pq):
    groups, lanes = mesh_shape
    prompts, width, part = pct.shape
    steps, seqs, heads, _ = rq.shape
    slots = REACH * CAPACITY
    bf, f32 = jnp.bfloat16, jnp.float32
    dma = pltpu.SemaphoreType.DMA
    anywhere = pl.BlockSpec(memory_space=pltpu.HBM)
    scalars = pl.BlockSpec(memory_space=pltpu.SMEM)
    plen, roff, rlen, sl, rct, rq, pct, pq = [
        pltpu.with_memory_space_constraint(x, pltpu.HBM) for x in (plen, roff, rlen, sl, rct, rq, pct, pq)
    ]
    return pl.pallas_call(
        functools.partial(kernel, groups, lanes),
        out_shape=(
            jax.ShapeDtypeStruct((steps, seqs, heads, LATENT_RANK), bf),
            jax.ShapeDtypeStruct((slots, heads, LATENT_RANK), bf),
            jax.ShapeDtypeStruct((slots, width, part), bf),
        ),
        in_specs=[scalars] * 3 + [anywhere] * 5,
        out_specs=(pl.BlockSpec(memory_space=pl.ANY),) * 3,
        scratch_shapes=[
            pltpu.VMEM(rct.shape, bf),
            pltpu.VMEM(rq.shape, bf),
            pltpu.VMEM(pct.shape, bf),
            pltpu.VMEM(sl.shape, bf),
            pltpu.VMEM((lanes,) + pq.shape, bf),
            pltpu.VMEM((128, width), bf),
            pltpu.VMEM((128, width), f32),
            pltpu.VMEM((lanes, prompts, heads, LATENT_RANK), bf),
            pltpu.VMEM((lanes, prompts, heads, LATENT_RANK), bf),
            pltpu.VMEM((lanes, heads, 128), f32),
            pltpu.VMEM((lanes, heads, 128), f32),
            pltpu.VMEM((prompts, heads, LATENT_RANK), bf),
            pltpu.VMEM((prompts, heads, LATENT_RANK), bf),
            pltpu.VMEM((heads, 128), f32),
            pltpu.VMEM((heads, 128), f32),
            pltpu.VMEM((CAPACITY, width, part), bf),
            pltpu.VMEM((REACH - 1, CAPACITY, width, part), bf),
            pltpu.VMEM((prompts, heads, LATENT_RANK), bf),
            pltpu.VMEM((REACH, CAPACITY, heads, LATENT_RANK), bf),
            pltpu.VMEM((steps, seqs, heads, LATENT_RANK), bf),
            dma((5,)),
            dma,
            dma((FAR, lanes // FAR)), dma((FAR, lanes // FAR)),
            dma((lanes,)), dma((lanes,)),
            dma((lanes,)), dma((lanes,)),
            dma((2,)), dma((2,)),
            dma((PIECES,)), dma((PIECES,)),
            dma((PIECES,)), dma((PIECES,)),
            dma((PIECES, REACH)), dma((PIECES, REACH)),
            dma((PIECES,)),
            dma((REACH,)), dma((REACH,)),
        ] + [pltpu.VMEM((prompts, width // PIECES, part), bf)] * PIECES,
        compiler_params=pltpu.CompilerParams(
            collective_id=0, has_side_effects=True, vmem_limit_bytes=40 * 1024 * 1024
        ),
        name="decode_and_migrate",
    )(plen, roff, rlen, sl, rct, rq, pct, pq)


def solution(mesh):
    mesh_shape = (mesh.shape["grp"], mesh.shape["head"])

    def body(
        resident_latent_cache, resident_len, resident_query, step_latent,
        prompt_cache, prompt_query, prompt_len, route_offset,
    ):
        ro, fo, ac = call(
            mesh_shape,
            prompt_len.T,
            route_offset[:, :, 0].T,
            resident_len,
            step_latent,
            jnp.swapaxes(resident_latent_cache, 1, 2),
            resident_query,
            jnp.swapaxes(prompt_cache, 1, 2),
            prompt_query,
        )
        return ro, fo[None], jnp.swapaxes(ac, 1, 2)[None]

    in_specs = (
        P("grp", None, None),
        P("grp", None),
        P(None, "grp", "head", None),
        P(None, "grp", None),
        P("grp", "head", None),
        P("grp", "head", None),
        P(),
        P(),
    )
    out_specs = (
        P(None, "grp", "head", None),
        P("grp", None, "head", None),
        P("grp", None, "head", None),
    )
    return jax.shard_map(body, mesh=mesh, in_specs=in_specs, out_specs=out_specs, check_vma=False)
```

```python
import functools

import jax
import jax.numpy as jnp
from jax import lax
from jax.experimental import pallas as pl
from jax.experimental.pallas import tpu as pltpu
from jax.sharding import PartitionSpec as P

LATENT_RANK = 512
REACH = 4
CAPACITY = 2
MESH = pl.DeviceIdType.MESH
SCALE = 192.0 ** (-0.5)
LOW = -1e30
NEW_ROWS = 16

FAR = 2
PIECES = 4

NN = (((1,), (0,)), ((), ()))
NT = (((1,), (1,)), ((), ()))


def matmul(a, b, dims):
    return lax.dot_general(a, b, dims, preferred_element_type=jnp.float32)


def kernel(
    groups, lanes,
    plen, roff, rlen, sl, rct, rq, pct, pq,
    ro, fo, ac,
    rctv, rqv, pctv, slv, qall, newk, newkf, obuf, rbuf, stat, rstat, xbuf, xrec, xstat, xrstat, hop, hopstat, near, picked, frows, fsend, rov,
    load_sem, out_sem, q_send, q_recv, o_send, o_recv, s_send, s_recv, x_send, x_recv, h_send, h_recv,
    w_send, w_recv, n_send, n_recv, p_send, p_recv, keep_sem, f_send, f_recv,
    *wholes,
):
    me = lax.axis_index("grp")
    lane = lax.axis_index("head")
    core = lax.rem(me, 2)
    prompts, width, part = pct.shape
    seqs = rct.shape[0]
    res_len = rct.shape[2]
    steps, _, heads, _ = rq.shape
    line = lanes // FAR
    piece = width // PIECES

    y, x = lane // FAR, lax.rem(lane, FAR)

    def on_lane(j, k):
        return (me, lax.rem(y + k, line) * FAR + lax.rem(x + j, FAR))

    def on_group(k):
        return (lax.rem(me + k + groups, groups), lane)

    direct = [(1, 0)] + [(0, k) for k in range(1, line)]
    others = direct + [(1, k) for k in range(1, line)]
    turn = lax.rem(me, groups // 2)
    first = turn < 2
    second = jnp.logical_and(turn >= 2, turn < 4)

    barrier = pltpu.get_barrier_semaphore()

    def greet(to):
        pl.semaphore_signal(barrier, inc=1, device_id=to, device_id_type=MESH)

    def beside(k):
        return (on_group(k)[0], on_lane(1, 0)[1])

    for k in range(REACH, 0, -1):
        greet(on_group(-k))
    for j, k in direct:
        greet(on_lane(j, k))
    pl.when(core == 0)(lambda: greet(on_group(1)))
    pl.when(first)(lambda: greet(on_group(2)))
    pl.when(second)(lambda: greet(beside(-2)))

    loads = [
        pltpu.make_async_copy(src, dst, load_sem.at[i])
        for i, (src, dst) in enumerate(((pct, pctv), (pq, qall.at[0]), (rct, rctv), (rq, rqv), (sl, slv)))
    ]
    for copy in loads:
        copy.start()

    extra = core + jnp.where(jnp.logical_or(first, second), 1, 0)
    pl.semaphore_wait(barrier, len(direct) + REACH + extra)

    def remote(src, dst, send, recv, to):
        return pltpu.make_async_remote_copy(
            src_ref=src, dst_ref=dst, send_sem=send, recv_sem=recv, device_id=to, device_id_type=MESH
        )

    def query_copy(j, k):
        slot, source = j * line + k, qall.at[j * line] if j and k else pq
        return remote(source, qall.at[slot], q_send.at[j, k], q_recv.at[j, k], on_lane(0 if k else j, k))

    q_copies = {(j, k): query_copy(j, k) for j, k in others}
    q_copies[1, 0].start()
    for k in range(1, line):
        q_copies[0, k].start()

    def latent(i):
        return pl.ds(i * piece, piece)

    w_copies = [
        remote(pct.at[:, latent(i)], wholes[i], w_send.at[i], w_recv.at[i], on_group(2))
        for i in range(PIECES)
    ]
    for copy in w_copies:
        copy.start()

    def places_of(group):
        offs = [roff[i, group] for i in range(prompts)]
        lens = [plen[i, group] - lane * part for i in range(prompts)]
        ranks = []
        for i in range(prompts):
            rank = jnp.int32(0)
            for i2 in range(i):
                rank = rank + jnp.where(offs[i2] == offs[i], 1, 0)
            ranks.append(rank)

        def pick(distance, place):
            index, length, filled = jnp.int32(0), jnp.int32(0), jnp.int32(0)
            for i in range(prompts):
                hit = jnp.logical_and(offs[i] == distance, ranks[i] == place)
                index = jnp.where(hit, i, index)
                length = jnp.where(hit, lens[i], length)
                filled = jnp.where(hit, 1, filled)
            return index, length, filled

        return lens, [[pick(d, r) for r in range(CAPACITY)] for d in range(REACH)]

    lens, slots = places_of(me)
    _, passing = places_of(lax.rem(me + groups - 2, groups))

    spots = lax.broadcasted_iota(jnp.int32, (piece, part), 1)

    def masked(ref, rows, slot):
        index, length, _ = slot
        block = ref[index, rows, :]
        return jnp.where(spots < length, block, jnp.zeros_like(block))

    n_copies = [
        remote(
            near.at[:, latent(i)], ac.at[pl.ds(0, CAPACITY), latent(i)],
            n_send.at[i], n_recv.at[i], on_group(1 - 2 * core),
        )
        for i in range(PIECES)
    ]
    loads[0].wait()

    @pl.when(core == 0)
    def _():
        for i in range(PIECES):
            for r in range(CAPACITY):
                near[r, latent(i), :] = masked(pctv, latent(i), slots[0][r])
            n_copies[i].start()

    p_copies, keeps = [], []
    for i in range(PIECES):
        for d in range(1, REACH):
            src, dst = picked.at[d - 1, :, latent(i)], ac.at[pl.ds(d * CAPACITY, CAPACITY), latent(i)]
            if d == 1:
                keeps.append(pltpu.make_async_copy(src, dst, keep_sem.at[i]))
            else:
                p_copies.append(remote(src, dst, p_send.at[i, d], p_recv.at[i, d], on_group(d - 1)))

    def pass_on(i):
        w_copies[i].wait_recv()
        for d in range(REACH - 1, 0, -1):
            for r in range(CAPACITY):
                picked[d - 1, r, latent(i), :] = masked(wholes[i], slice(None), passing[d][r])
            if d == 1:
                keeps[i].start()
            else:
                p_copies[i * (REACH - 2) + d - 2].start()

        @pl.when(core == 1)
        def _():
            for r in range(CAPACITY):
                near[r, latent(i), :] = masked(wholes[i], slice(None), passing[0][r])
            n_copies[i].start()

    def pass_when(*pieces, where):
        for i in pieces:
            pl.when(where)(functools.partial(pass_on, i))

    loads[4].wait()
    newkf[...] = jnp.zeros_like(newkf)
    for u in range(steps):
        step_rows = slv[u].astype(jnp.float32)
        for s in range(seqs):
            newkf[pl.ds(s * NEW_ROWS + u, 1), :] = step_rows[s:s + 1, :]
    newk[...] = newkf[...].astype(jnp.bfloat16)
    loads[2].wait()
    loads[3].wait()

    def resident(s):
        count = steps * heads
        query = rqv[:, s].reshape(count, width)
        fresh = newk.shape[0]
        old = matmul(query, rctv[s], NN) * SCALE
        new = matmul(query, newk[...], NT) * SCALE
        old_live = lax.broadcasted_iota(jnp.int32, (count, res_len), 1) < rlen[0, s]
        step = lax.broadcasted_iota(jnp.int32, (count, fresh), 0) // heads
        token = lax.broadcasted_iota(jnp.int32, (count, fresh), 1) - s * NEW_ROWS
        new_live = jnp.logical_and(token >= 0, token <= step)
        old = jnp.where(old_live, old, LOW)
        new = jnp.where(new_live, new, LOW)
        top = jnp.maximum(jnp.max(old, 1, keepdims=True), jnp.max(new, 1, keepdims=True))
        old = jnp.where(old_live, jnp.exp(old - top), 0.0)
        new = jnp.where(new_live, jnp.exp(new - top), 0.0)
        total = jnp.sum(old, 1, keepdims=True) + jnp.sum(new, 1, keepdims=True)
        mixed = matmul(old.astype(jnp.bfloat16), rctv[s, :LATENT_RANK, :], NT)
        mixed = mixed + matmul(new.astype(jnp.bfloat16), newk[:, :LATENT_RANK], NN)
        rov[:, s] = (mixed / total).astype(jnp.bfloat16).reshape(steps, heads, LATENT_RANK)

    q_copies[1, 0].wait_recv()
    for k in range(1, line):
        q_copies[1, k].start()

    for s in range(seqs // 2):
        resident(s)

    side = line * heads
    column = lax.broadcasted_iota(jnp.int32, (side, 128), 1)
    position = lax.broadcasted_iota(jnp.int32, (side, part), 1)
    o_copies = {}

    def attend(j):
        stats = jnp.zeros((side, 128), jnp.float32)
        for p in range(prompts):
            query = qall[pl.ds(j * line, line), p].reshape(side, width)
            live = position < lens[p]
            scores = jnp.where(live, matmul(query, pctv[p], NN) * SCALE, LOW)
            top = jnp.max(scores, 1, keepdims=True)
            weights = jnp.where(live, jnp.exp(scores - top), 0.0)
            total = jnp.sum(weights, 1, keepdims=True)
            mixed = matmul(weights.astype(jnp.bfloat16), pctv[p, :LATENT_RANK, :], NT)
            obuf[pl.ds(j * line, line), p] = mixed.astype(jnp.bfloat16).reshape(line, heads, LATENT_RANK)
            stats = jnp.where(column == 2 * p, top, stats)
            stats = jnp.where(column == 2 * p + 1, total, stats)
        stat[pl.ds(j * line, line)] = stats.reshape(line, heads, 128)
        o_copies[j] = []
        for k in range(1, line):
            slot, to = j * line + k, on_lane(0, line - k)
            o_copies[j].append(remote(obuf.at[slot], rbuf.at[slot], o_send.at[slot], o_recv.at[slot], to))
            o_copies[j].append(remote(stat.at[slot], rstat.at[slot], s_send.at[slot], s_recv.at[slot], to))
        for copy in o_copies[j]:
            copy.start()

    def merged(p, parts):
        tops = [where[:, 2 * p:2 * p + 1] for where, _ in parts]
        sums = [where[:, 2 * p + 1:2 * p + 2] for where, _ in parts]
        top = functools.reduce(jnp.maximum, tops)
        total = jnp.zeros_like(top)
        mixed = jnp.zeros((heads, LATENT_RANK), jnp.float32)
        for own_top, own_sum, (_, values) in zip(tops, sums, parts):
            factor = jnp.exp(own_top - top)
            total = total + factor * own_sum
            mixed = mixed + factor * values[p].astype(jnp.float32)
        return top, total, mixed

    def parts_of(j):
        slots_of = [j * line + k for k in range(line)]
        return [
            ((stat if k == 0 else rstat).at[slot], (obuf if k == 0 else rbuf).at[slot])
            for k, slot in enumerate(slots_of)
        ]

    rest = jnp.logical_not(first)
    pass_when(0, 1, where=rest)
    loads[1].wait()
    for k in range(1, line):
        q_copies[0, k].wait_recv()
    attend(0)
    for k in range(1, line):
        q_copies[1, k].wait_recv()
    attend(1)

    pass_when(2, where=rest)
    for copy in o_copies[1]:
        copy.wait_recv()
    crossing = jnp.zeros((heads, 128), jnp.float32)
    lanes_of = lax.broadcasted_iota(jnp.int32, (heads, 128), 1)
    for p in range(prompts):
        top, total, mixed = merged(p, parts_of(1))
        xbuf[p] = mixed.astype(jnp.bfloat16)
        crossing = jnp.where(lanes_of == 2 * p, top, crossing)
        crossing = jnp.where(lanes_of == 2 * p + 1, total, crossing)
    xstat[...] = crossing
    crossings = ((xbuf, xrec, hop), (xstat, xrstat, hopstat))
    x_copies, out_copies, back_copies = [], [], []
    for i, (src, dst, via) in enumerate(crossings):
        x_copies.append(remote(src, dst, x_send.at[i], x_recv.at[i], on_lane(1, 0)))
        out_copies.append(remote(src, via, x_send.at[i], h_recv.at[i], beside(2)))
        back_copies.append(remote(via, dst, h_send.at[i], x_recv.at[i], on_group(-2)))

    @pl.when(first)
    def _():
        for copy in out_copies:
            copy.start()

    @pl.when(jnp.logical_not(first))
    def _():
        for copy in x_copies:
            copy.start()

    for s in range(seqs // 2, seqs):
        resident(s)
    pass_when(*range(PIECES), where=first)
    done = pltpu.make_async_copy(rov, ro, out_sem)
    done.start()

    for copy in o_copies[0] + x_copies:
        copy.wait_recv()
    for p in range(prompts):
        _, total, mixed = merged(p, parts_of(0) + [(xrstat, xrec)])
        frows[p] = (mixed / jnp.maximum(total, 1.0)).astype(jnp.bfloat16)

    spread = lax.broadcasted_iota(jnp.int32, (heads, LATENT_RANK), 0)
    f_copies = []
    for d in range(REACH - 1, -1, -1):
        for r in range(CAPACITY):
            index, _, filled = slots[d][r]
            block = frows[index]
            fsend[d, r] = jnp.where(spread < filled * heads, block, jnp.zeros_like(block))
        copy = remote(
            fsend.at[d], fo.at[pl.ds(d * CAPACITY, CAPACITY)], f_send.at[d], f_recv.at[d], on_group(d + 1)
        )
        copy.start()
        f_copies.append(copy)

    @pl.when(second)
    def _():
        for out, back in zip(out_copies, back_copies):
            out.wait_recv()
            back.start()

    pass_when(3, where=rest)

    @pl.when(second)
    def _():
        for back in back_copies:
            back.wait_send()

    for copy in [done] + keeps:
        copy.wait()
    for copies in (q_copies.values(), o_copies[0], o_copies[1], x_copies, w_copies):
        for copy in copies:
            copy.wait_send()
    for copies in (n_copies, p_copies, f_copies):
        for copy in copies:
            copy.wait_send()
            copy.wait_recv()


def call(mesh_shape, plen, roff, rlen, sl, rct, rq, pct, pq):
    groups, lanes = mesh_shape
    prompts, width, part = pct.shape
    steps, seqs, heads, _ = rq.shape
    slots = REACH * CAPACITY
    bf, f32 = jnp.bfloat16, jnp.float32
    dma = pltpu.SemaphoreType.DMA
    anywhere = pl.BlockSpec(memory_space=pltpu.HBM)
    scalars = pl.BlockSpec(memory_space=pltpu.SMEM)
    plen, roff, rlen, sl, rct, rq, pct, pq = [
        pltpu.with_memory_space_constraint(x, pltpu.HBM) for x in (plen, roff, rlen, sl, rct, rq, pct, pq)
    ]
    return pl.pallas_call(
        functools.partial(kernel, groups, lanes),
        out_shape=(
            jax.ShapeDtypeStruct((steps, seqs, heads, LATENT_RANK), bf),
            jax.ShapeDtypeStruct((slots, heads, LATENT_RANK), bf),
            jax.ShapeDtypeStruct((slots, width, part), bf),
        ),
        in_specs=[scalars] * 3 + [anywhere] * 5,
        out_specs=(pl.BlockSpec(memory_space=pl.ANY),) * 3,
        scratch_shapes=[
            pltpu.VMEM(rct.shape, bf),
            pltpu.VMEM(rq.shape, bf),
            pltpu.VMEM(pct.shape, bf),
            pltpu.VMEM(sl.shape, bf),
            pltpu.VMEM((lanes,) + pq.shape, bf),
            pltpu.VMEM((128, width), bf),
            pltpu.VMEM((128, width), f32),
            pltpu.VMEM((lanes, prompts, heads, LATENT_RANK), bf),
            pltpu.VMEM((lanes, prompts, heads, LATENT_RANK), bf),
            pltpu.VMEM((lanes, heads, 128), f32),
            pltpu.VMEM((lanes, heads, 128), f32),
            pltpu.VMEM((prompts, heads, LATENT_RANK), bf),
            pltpu.VMEM((prompts, heads, LATENT_RANK), bf),
            pltpu.VMEM((heads, 128), f32),
            pltpu.VMEM((heads, 128), f32),
            pltpu.VMEM((prompts, heads, LATENT_RANK), bf),
            pltpu.VMEM((heads, 128), f32),
            pltpu.VMEM((CAPACITY, width, part), bf),
            pltpu.VMEM((REACH - 1, CAPACITY, width, part), bf),
            pltpu.VMEM((prompts, heads, LATENT_RANK), bf),
            pltpu.VMEM((REACH, CAPACITY, heads, LATENT_RANK), bf),
            pltpu.VMEM((steps, seqs, heads, LATENT_RANK), bf),
            dma((5,)),
            dma,
            dma((FAR, lanes // FAR)), dma((FAR, lanes // FAR)),
            dma((lanes,)), dma((lanes,)),
            dma((lanes,)), dma((lanes,)),
            dma((2,)), dma((2,)),
            dma((2,)), dma((2,)),
            dma((PIECES,)), dma((PIECES,)),
            dma((PIECES,)), dma((PIECES,)),
            dma((PIECES, REACH)), dma((PIECES, REACH)),
            dma((PIECES,)),
            dma((REACH,)), dma((REACH,)),
        ] + [pltpu.VMEM((prompts, width // PIECES, part), bf)] * PIECES,
        compiler_params=pltpu.CompilerParams(
            collective_id=0, has_side_effects=True, vmem_limit_bytes=40 * 1024 * 1024
        ),
        name="decode_and_migrate",
    )(plen, roff, rlen, sl, rct, rq, pct, pq)


def solution(mesh):
    mesh_shape = (mesh.shape["grp"], mesh.shape["head"])

    def body(
        resident_latent_cache, resident_len, resident_query, step_latent,
        prompt_cache, prompt_query, prompt_len, route_offset,
    ):
        ro, fo, ac = call(
            mesh_shape,
            prompt_len.T,
            route_offset[:, :, 0].T,
            resident_len,
            step_latent,
            jnp.swapaxes(resident_latent_cache, 1, 2),
            resident_query,
            jnp.swapaxes(prompt_cache, 1, 2),
            prompt_query,
        )
        return ro, fo[None], jnp.swapaxes(ac, 1, 2)[None]

    in_specs = (
        P("grp", None, None),
        P("grp", None),
        P(None, "grp", "head", None),
        P(None, "grp", None),
        P("grp", "head", None),
        P("grp", "head", None),
        P(),
        P(),
    )
    out_specs = (
        P(None, "grp", "head", None),
        P("grp", None, "head", None),
        P("grp", None, "head", None),
    )
    return jax.shard_map(body, mesh=mesh, in_specs=in_specs, out_specs=out_specs, check_vma=False)
```

```python
import functools

import jax
import jax.numpy as jnp
from jax import lax
from jax.experimental import pallas as pl
from jax.experimental.pallas import tpu as pltpu
from jax.sharding import PartitionSpec as P

LATENT_RANK = 512
REACH = 4
CAPACITY = 2
MESH = pl.DeviceIdType.MESH
SCALE = 192.0 ** (-0.5)
LOW = -1e30
NEW_ROWS = 16

FAR = 2
PIECES = 4

NN = (((1,), (0,)), ((), ()))
NT = (((1,), (1,)), ((), ()))


def matmul(a, b, dims):
    return lax.dot_general(a, b, dims, preferred_element_type=jnp.float32)


def kernel(
    groups, lanes,
    plen_hbm, roff_hbm, rlen_hbm, sl, rct, rq, pct, pq,
    ro, fo, ac,
    plen, roff, rlen,
    rctv, rqv, pctv, slv, qall, newk, newkf, obuf, rbuf, stat, rstat, xbuf, xrec, xstat, xrstat, hop, hopstat, near, picked, frows, fsend, rov,
    load_sem, out_sem, q_send, q_recv, o_send, o_recv, s_send, s_recv, x_send, x_recv, h_send, h_recv,
    w_send, w_recv, n_send, n_recv, p_send, p_recv, keep_sem, f_send, f_recv,
    *wholes,
):
    me = lax.axis_index("grp")
    lane = lax.axis_index("head")
    core = lax.rem(me, 2)
    prompts, width, part = pct.shape
    seqs = rct.shape[0]
    res_len = rct.shape[2]
    steps, _, heads, _ = rq.shape
    line = lanes // FAR
    piece = width // PIECES

    y, x = lane // FAR, lax.rem(lane, FAR)

    def on_lane(j, k):
        return (me, lax.rem(y + k, line) * FAR + lax.rem(x + j, FAR))

    def on_group(k):
        return (lax.rem(me + k + groups, groups), lane)

    direct = [(1, 0)] + [(0, k) for k in range(1, line)]
    others = direct + [(1, k) for k in range(1, line)]
    turn = lax.rem(me, groups // 2)
    first = turn < 2
    second = jnp.logical_and(turn >= 2, turn < 4)

    barrier = pltpu.get_barrier_semaphore()

    def greet(to):
        pl.semaphore_signal(barrier, inc=1, device_id=to, device_id_type=MESH)

    def beside(k):
        return (on_group(k)[0], on_lane(1, 0)[1])

    for k in range(REACH, 0, -1):
        greet(on_group(-k))
    for j, k in direct:
        greet(on_lane(j, k))
    pl.when(core == 0)(lambda: greet(on_group(1)))
    pl.when(first)(lambda: greet(on_group(2)))
    pl.when(second)(lambda: greet(beside(-2)))

    loads = [
        pltpu.make_async_copy(src, dst, load_sem.at[i])
        for i, (src, dst) in enumerate(((pct, pctv), (pq, qall.at[0]), (rct, rctv), (rq, rqv), (sl, slv),
                                    (plen_hbm, plen), (roff_hbm, roff), (rlen_hbm, rlen)))
    ]
    for copy in loads:
        copy.start()

    extra = core + jnp.where(jnp.logical_or(first, second), 1, 0)
    pl.semaphore_wait(barrier, len(direct) + REACH + extra)

    def remote(src, dst, send, recv, to):
        return pltpu.make_async_remote_copy(
            src_ref=src, dst_ref=dst, send_sem=send, recv_sem=recv, device_id=to, device_id_type=MESH
        )

    def query_copy(j, k):
        slot, source = j * line + k, qall.at[j * line] if j and k else pq
        return remote(source, qall.at[slot], q_send.at[j, k], q_recv.at[j, k], on_lane(0 if k else j, k))

    q_copies = {(j, k): query_copy(j, k) for j, k in others}
    q_copies[1, 0].start()
    for k in range(1, line):
        q_copies[0, k].start()

    def latent(i):
        return pl.ds(i * piece, piece)

    w_copies = [
        remote(pct.at[:, latent(i)], wholes[i], w_send.at[i], w_recv.at[i], on_group(2))
        for i in range(PIECES)
    ]
    for copy in w_copies:
        copy.start()

    def places_of(group):
        offs = [roff[i, group] for i in range(prompts)]
        lens = [plen[i, group] - lane * part for i in range(prompts)]
        ranks = []
        for i in range(prompts):
            rank = jnp.int32(0)
            for i2 in range(i):
                rank = rank + jnp.where(offs[i2] == offs[i], 1, 0)
            ranks.append(rank)

        def pick(distance, place):
            index, length, filled = jnp.int32(0), jnp.int32(0), jnp.int32(0)
            for i in range(prompts):
                hit = jnp.logical_and(offs[i] == distance, ranks[i] == place)
                index = jnp.where(hit, i, index)
                length = jnp.where(hit, lens[i], length)
                filled = jnp.where(hit, 1, filled)
            return index, length, filled

        return lens, [[pick(d, r) for r in range(CAPACITY)] for d in range(REACH)]

    for copy in loads[5:]:
        copy.wait()
    lens, slots = places_of(me)
    _, passing = places_of(lax.rem(me + groups - 2, groups))

    spots = lax.broadcasted_iota(jnp.int32, (piece, part), 1)

    def masked(ref, rows, slot):
        index, length, _ = slot
        block = ref[index, rows, :]
        return jnp.where(spots < length, block, jnp.zeros_like(block))

    n_copies = [
        remote(
            near.at[:, latent(i)], ac.at[pl.ds(0, CAPACITY), latent(i)],
            n_send.at[i], n_recv.at[i], on_group(1 - 2 * core),
        )
        for i in range(PIECES)
    ]
    loads[0].wait()

    @pl.when(core == 0)
    def _():
        for i in range(PIECES):
            for r in range(CAPACITY):
                near[r, latent(i), :] = masked(pctv, latent(i), slots[0][r])
            n_copies[i].start()

    p_copies, keeps = [], []
    for i in range(PIECES):
        for d in range(1, REACH):
            src, dst = picked.at[d - 1, :, latent(i)], ac.at[pl.ds(d * CAPACITY, CAPACITY), latent(i)]
            if d == 1:
                keeps.append(pltpu.make_async_copy(src, dst, keep_sem.at[i]))
            else:
                p_copies.append(remote(src, dst, p_send.at[i, d], p_recv.at[i, d], on_group(d - 1)))

    def pass_on(i):
        w_copies[i].wait_recv()
        for d in range(REACH - 1, 0, -1):
            for r in range(CAPACITY):
                picked[d - 1, r, latent(i), :] = masked(wholes[i], slice(None), passing[d][r])
            if d == 1:
                keeps[i].start()
            else:
                p_copies[i * (REACH - 2) + d - 2].start()

        @pl.when(core == 1)
        def _():
            for r in range(CAPACITY):
                near[r, latent(i), :] = masked(wholes[i], slice(None), passing[0][r])
            n_copies[i].start()

    def pass_when(*pieces, where):
        for i in pieces:
            pl.when(where)(functools.partial(pass_on, i))

    loads[4].wait()
    newkf[...] = jnp.zeros_like(newkf)
    for u in range(steps):
        step_rows = slv[u].astype(jnp.float32)
        for s in range(seqs):
            newkf[pl.ds(s * NEW_ROWS + u, 1), :] = step_rows[s:s + 1, :]
    newk[...] = newkf[...].astype(jnp.bfloat16)
    loads[2].wait()
    loads[3].wait()

    def resident(s):
        count = steps * heads
        query = rqv[:, s].reshape(count, width)
        fresh = newk.shape[0]
        old = matmul(query, rctv[s], NN) * SCALE
        new = matmul(query, newk[...], NT) * SCALE
        old_live = lax.broadcasted_iota(jnp.int32, (count, res_len), 1) < rlen[0, s]
        step = lax.broadcasted_iota(jnp.int32, (count, fresh), 0) // heads
        token = lax.broadcasted_iota(jnp.int32, (count, fresh), 1) - s * NEW_ROWS
        new_live = jnp.logical_and(token >= 0, token <= step)
        old = jnp.where(old_live, old, LOW)
        new = jnp.where(new_live, new, LOW)
        top = jnp.maximum(jnp.max(old, 1, keepdims=True), jnp.max(new, 1, keepdims=True))
        old = jnp.where(old_live, jnp.exp(old - top), 0.0)
        new = jnp.where(new_live, jnp.exp(new - top), 0.0)
        total = jnp.sum(old, 1, keepdims=True) + jnp.sum(new, 1, keepdims=True)
        mixed = matmul(old.astype(jnp.bfloat16), rctv[s, :LATENT_RANK, :], NT)
        mixed = mixed + matmul(new.astype(jnp.bfloat16), newk[:, :LATENT_RANK], NN)
        rov[:, s] = (mixed / total).astype(jnp.bfloat16).reshape(steps, heads, LATENT_RANK)

    q_copies[1, 0].wait_recv()
    for k in range(1, line):
        q_copies[1, k].start()

    for s in range(seqs // 2):
        resident(s)

    side = line * heads
    column = lax.broadcasted_iota(jnp.int32, (side, 128), 1)
    position = lax.broadcasted_iota(jnp.int32, (side, part), 1)
    o_copies = {}

    def attend(j):
        stats = jnp.zeros((side, 128), jnp.float32)
        for p in range(prompts):
            query = qall[pl.ds(j * line, line), p].reshape(side, width)
            live = position < lens[p]
            scores = jnp.where(live, matmul(query, pctv[p], NN) * SCALE, LOW)
            top = jnp.max(scores, 1, keepdims=True)
            weights = jnp.where(live, jnp.exp(scores - top), 0.0)
            total = jnp.sum(weights, 1, keepdims=True)
            mixed = matmul(weights.astype(jnp.bfloat16), pctv[p, :LATENT_RANK, :], NT)
            obuf[pl.ds(j * line, line), p] = mixed.astype(jnp.bfloat16).reshape(line, heads, LATENT_RANK)
            stats = jnp.where(column == 2 * p, top, stats)
            stats = jnp.where(column == 2 * p + 1, total, stats)
        stat[pl.ds(j * line, line)] = stats.reshape(line, heads, 128)
        o_copies[j] = []
        for k in range(1, line):
            slot, to = j * line + k, on_lane(0, line - k)
            o_copies[j].append(remote(obuf.at[slot], rbuf.at[slot], o_send.at[slot], o_recv.at[slot], to))
            o_copies[j].append(remote(stat.at[slot], rstat.at[slot], s_send.at[slot], s_recv.at[slot], to))
        for copy in o_copies[j]:
            copy.start()

    def merged(p, parts):
        tops = [where[:, 2 * p:2 * p + 1] for where, _ in parts]
        sums = [where[:, 2 * p + 1:2 * p + 2] for where, _ in parts]
        top = functools.reduce(jnp.maximum, tops)
        total = jnp.zeros_like(top)
        mixed = jnp.zeros((heads, LATENT_RANK), jnp.float32)
        for own_top, own_sum, (_, values) in zip(tops, sums, parts):
            factor = jnp.exp(own_top - top)
            total = total + factor * own_sum
            mixed = mixed + factor * values[p].astype(jnp.float32)
        return top, total, mixed

    def parts_of(j):
        slots_of = [j * line + k for k in range(line)]
        return [
            ((stat if k == 0 else rstat).at[slot], (obuf if k == 0 else rbuf).at[slot])
            for k, slot in enumerate(slots_of)
        ]

    rest = jnp.logical_not(first)
    pass_when(0, 1, where=rest)
    loads[1].wait()
    for k in range(1, line):
        q_copies[0, k].wait_recv()
    attend(0)
    for k in range(1, line):
        q_copies[1, k].wait_recv()
    attend(1)

    pass_when(2, where=rest)
    for copy in o_copies[1]:
        copy.wait_recv()
    crossing = jnp.zeros((heads, 128), jnp.float32)
    lanes_of = lax.broadcasted_iota(jnp.int32, (heads, 128), 1)
    for p in range(prompts):
        top, total, mixed = merged(p, parts_of(1))
        xbuf[p] = mixed.astype(jnp.bfloat16)
        crossing = jnp.where(lanes_of == 2 * p, top, crossing)
        crossing = jnp.where(lanes_of == 2 * p + 1, total, crossing)
    xstat[...] = crossing
    crossings = ((xbuf, xrec, hop), (xstat, xrstat, hopstat))
    x_copies, out_copies, back_copies = [], [], []
    for i, (src, dst, via) in enumerate(crossings):
        x_copies.append(remote(src, dst, x_send.at[i], x_recv.at[i], on_lane(1, 0)))
        out_copies.append(remote(src, via, x_send.at[i], h_recv.at[i], beside(2)))
        back_copies.append(remote(via, dst, h_send.at[i], x_recv.at[i], on_group(-2)))

    @pl.when(first)
    def _():
        for copy in out_copies:
            copy.start()

    @pl.when(jnp.logical_not(first))
    def _():
        for copy in x_copies:
            copy.start()

    for s in range(seqs // 2, seqs):
        resident(s)
    pass_when(*range(PIECES), where=first)
    done = pltpu.make_async_copy(rov, ro, out_sem)
    done.start()

    for copy in o_copies[0] + x_copies:
        copy.wait_recv()
    for p in range(prompts):
        _, total, mixed = merged(p, parts_of(0) + [(xrstat, xrec)])
        frows[p] = (mixed / jnp.maximum(total, 1.0)).astype(jnp.bfloat16)

    spread = lax.broadcasted_iota(jnp.int32, (heads, LATENT_RANK), 0)
    f_copies = []
    for d in range(REACH - 1, -1, -1):
        for r in range(CAPACITY):
            index, _, filled = slots[d][r]
            block = frows[index]
            fsend[d, r] = jnp.where(spread < filled * heads, block, jnp.zeros_like(block))
        copy = remote(
            fsend.at[d], fo.at[pl.ds(d * CAPACITY, CAPACITY)], f_send.at[d], f_recv.at[d], on_group(d + 1)
        )
        copy.start()
        f_copies.append(copy)

    @pl.when(second)
    def _():
        for out, back in zip(out_copies, back_copies):
            out.wait_recv()
            back.start()

    pass_when(3, where=rest)

    @pl.when(second)
    def _():
        for back in back_copies:
            back.wait_send()

    for copy in [done] + keeps:
        copy.wait()
    for copies in (q_copies.values(), o_copies[0], o_copies[1], x_copies, w_copies):
        for copy in copies:
            copy.wait_send()
    for copies in (n_copies, p_copies, f_copies):
        for copy in copies:
            copy.wait_send()
            copy.wait_recv()


def call(mesh_shape, plen, roff, rlen, sl, rct, rq, pct, pq):
    groups, lanes = mesh_shape
    prompts, width, part = pct.shape
    steps, seqs, heads, _ = rq.shape
    slots = REACH * CAPACITY
    bf, f32 = jnp.bfloat16, jnp.float32
    dma = pltpu.SemaphoreType.DMA
    anywhere = pl.BlockSpec(memory_space=pltpu.HBM)
    plen, roff, rlen, sl, rct, rq, pct, pq = [
        pltpu.with_memory_space_constraint(x, pltpu.HBM) for x in (plen, roff, rlen, sl, rct, rq, pct, pq)
    ]
    return pl.pallas_call(
        functools.partial(kernel, groups, lanes),
        out_shape=(
            jax.ShapeDtypeStruct((steps, seqs, heads, LATENT_RANK), bf),
            jax.ShapeDtypeStruct((slots, heads, LATENT_RANK), bf),
            jax.ShapeDtypeStruct((slots, width, part), bf),
        ),
        in_specs=[anywhere] * 8,
        out_specs=(pl.BlockSpec(memory_space=pl.ANY),) * 3,
        scratch_shapes=[
            pltpu.SMEM(plen.shape, jnp.int32),
            pltpu.SMEM(roff.shape, jnp.int32),
            pltpu.SMEM(rlen.shape, jnp.int32),
            pltpu.VMEM(rct.shape, bf),
            pltpu.VMEM(rq.shape, bf),
            pltpu.VMEM(pct.shape, bf),
            pltpu.VMEM(sl.shape, bf),
            pltpu.VMEM((lanes,) + pq.shape, bf),
            pltpu.VMEM((128, width), bf),
            pltpu.VMEM((128, width), f32),
            pltpu.VMEM((lanes, prompts, heads, LATENT_RANK), bf),
            pltpu.VMEM((lanes, prompts, heads, LATENT_RANK), bf),
            pltpu.VMEM((lanes, heads, 128), f32),
            pltpu.VMEM((lanes, heads, 128), f32),
            pltpu.VMEM((prompts, heads, LATENT_RANK), bf),
            pltpu.VMEM((prompts, heads, LATENT_RANK), bf),
            pltpu.VMEM((heads, 128), f32),
            pltpu.VMEM((heads, 128), f32),
            pltpu.VMEM((prompts, heads, LATENT_RANK), bf),
            pltpu.VMEM((heads, 128), f32),
            pltpu.VMEM((CAPACITY, width, part), bf),
            pltpu.VMEM((REACH - 1, CAPACITY, width, part), bf),
            pltpu.VMEM((prompts, heads, LATENT_RANK), bf),
            pltpu.VMEM((REACH, CAPACITY, heads, LATENT_RANK), bf),
            pltpu.VMEM((steps, seqs, heads, LATENT_RANK), bf),
            dma((8,)),
            dma,
            dma((FAR, lanes // FAR)), dma((FAR, lanes // FAR)),
            dma((lanes,)), dma((lanes,)),
            dma((lanes,)), dma((lanes,)),
            dma((2,)), dma((2,)),
            dma((2,)), dma((2,)),
            dma((PIECES,)), dma((PIECES,)),
            dma((PIECES,)), dma((PIECES,)),
            dma((PIECES, REACH)), dma((PIECES, REACH)),
            dma((PIECES,)),
            dma((REACH,)), dma((REACH,)),
        ] + [pltpu.VMEM((prompts, width // PIECES, part), bf)] * PIECES,
        compiler_params=pltpu.CompilerParams(
            collective_id=0, has_side_effects=True, vmem_limit_bytes=40 * 1024 * 1024
        ),
        name="decode_and_migrate",
    )(plen, roff, rlen, sl, rct, rq, pct, pq)


def writer(*refs):
    count = len(refs) // 2
    sems = refs[-1]
    copies = [pltpu.make_async_copy(refs[i], refs[count + i], sems.at[i]) for i in range(count)]
    for copy in copies:
        copy.start()
    for copy in copies:
        copy.wait()


def write_out(*arrays):
    arrays = [pltpu.with_memory_space_constraint(x, pltpu.VMEM) for x in arrays]
    return pl.pallas_call(
        writer,
        out_shape=tuple(jax.ShapeDtypeStruct(x.shape, x.dtype) for x in arrays),
        in_specs=[pl.BlockSpec(memory_space=pltpu.VMEM)] * len(arrays),
        out_specs=(pl.BlockSpec(memory_space=pltpu.HBM),) * len(arrays),
        scratch_shapes=[pltpu.SemaphoreType.DMA((len(arrays),))],
        name="write_out",
    )(*arrays)


def solution(mesh):
    mesh_shape = (mesh.shape["grp"], mesh.shape["head"])

    def body(
        resident_latent_cache, resident_len, resident_query, step_latent,
        prompt_cache, prompt_query, prompt_len, route_offset,
    ):
        ro, fo, ac = write_out(*call(
            mesh_shape,
            prompt_len.T,
            route_offset[:, :, 0].T,
            resident_len,
            step_latent,
            jnp.swapaxes(resident_latent_cache, 1, 2),
            resident_query,
            jnp.swapaxes(prompt_cache, 1, 2),
            prompt_query,
        ))
        return ro, fo[None], jnp.swapaxes(ac, 1, 2)[None]

    in_specs = (
        P("grp", None, None),
        P("grp", None),
        P(None, "grp", "head", None),
        P(None, "grp", None),
        P("grp", "head", None),
        P("grp", "head", None),
        P(),
        P(),
    )
    out_specs = (
        P(None, "grp", "head", None),
        P("grp", None, "head", None),
        P("grp", None, "head", None),
    )
    return jax.shard_map(body, mesh=mesh, in_specs=in_specs, out_specs=out_specs, check_vma=False)
```

```python
import functools

import jax
import jax.numpy as jnp
from jax import lax
from jax.experimental import pallas as pl
from jax.experimental.pallas import tpu as pltpu
from jax.sharding import PartitionSpec as P

LATENT_RANK = 512
REACH = 4
CAPACITY = 2
MESH = pl.DeviceIdType.MESH
SCALE = 192.0 ** (-0.5)
LOW = -1e30
NEW_ROWS = 16

FAR = 2
HALVES = 2
PIECES = 4

NN = (((1,), (0,)), ((), ()))
NT = (((1,), (1,)), ((), ()))


def matmul(a, b, dims):
    return lax.dot_general(a, b, dims, preferred_element_type=jnp.float32)


def kernel(
    groups, lanes,
    plen_hbm, roff_hbm, rlen_hbm, sl, rct, rq, pct, pq,
    ro, fo, ac,
    plen, roff, rlen,
    rctv, rqv, pctv, slv, qall, newk, newkf, obuf, rbuf, stat, rstat, xbuf, xrec, xstat, xrstat, mbuf, mstat, hop, hopstat, given, via, near, picked, frows, fsend, rov,
    load_sem, out_sem, q_send, q_recv, o_send, o_recv, s_send, s_recv, x_send, x_recv, h_send, h_recv,
    w_send, w_recv, n_send, n_recv, p_send, p_recv, keep_sem, f_send, f_recv, v_send, v_recv, b_send,
    *wholes,
):
    me = lax.axis_index("grp")
    lane = lax.axis_index("head")
    core = lax.rem(me, 2)
    prompts, width, part = pct.shape
    seqs = rct.shape[0]
    res_len = rct.shape[2]
    steps, _, heads, _ = rq.shape
    line = lanes // FAR
    piece = width // PIECES

    y, x = lane // FAR, lax.rem(lane, FAR)

    def on_lane(j, k):
        return (me, lax.rem(y + k, line) * FAR + lax.rem(x + j, FAR))

    def on_group(k):
        return (lax.rem(me + k + groups, groups), lane)

    direct = [(1, 0)] + [(0, k) for k in range(1, line)]
    others = direct + [(1, k) for k in range(1, line)]
    turn = lax.rem(me, groups // 2)
    first = turn < 2
    second = jnp.logical_and(turn >= 2, turn < 4)
    mid = (groups // 2 - 4) // 4 * 2
    giver, bearer, taker = turn == groups // 2 - 4, turn == mid, turn == 0
    spared = turn == groups // 2 - 2

    barrier = pltpu.get_barrier_semaphore()

    def greet(to):
        pl.semaphore_signal(barrier, inc=1, device_id=to, device_id_type=MESH)

    def beside(k):
        return (on_group(k)[0], on_lane(1, 0)[1])

    for k in range(REACH, 0, -1):
        greet(on_group(-k))
    for j, k in direct:
        greet(on_lane(j, k))
    pl.when(core == 0)(lambda: greet(on_group(1)))
    pl.when(taker)(lambda: greet(on_group(mid)))
    pl.when(bearer)(lambda: greet(on_group(-mid - 4)))
    pl.when(first)(lambda: greet(on_group(2)))
    pl.when(second)(lambda: greet(beside(-2)))

    loads = [
        pltpu.make_async_copy(src, dst, load_sem.at[i])
        for i, (src, dst) in enumerate(((pct, pctv), (pq, qall.at[0]), (rct, rctv), (rq, rqv), (sl, slv),
                                    (plen_hbm, plen), (roff_hbm, roff), (rlen_hbm, rlen)))
    ]
    for copy in loads:
        copy.start()

    extra = core + jnp.where(jnp.logical_or(first, second), 1, 0)
    extra = extra + jnp.where(jnp.logical_or(giver, bearer), 1, 0)
    pl.semaphore_wait(barrier, len(direct) + REACH + extra)

    def remote(src, dst, send, recv, to):
        return pltpu.make_async_remote_copy(
            src_ref=src, dst_ref=dst, send_sem=send, recv_sem=recv, device_id=to, device_id_type=MESH
        )

    half = prompts // HALVES

    def query_copy(j, k, h):
        slot, held = j * line + k, pl.ds(h * half, half)
        source = qall.at[j * line, held] if j and k else pq.at[held]
        return remote(source, qall.at[slot, held], q_send.at[slot, h], q_recv.at[slot, h], on_lane(0 if k else j, k))

    q_copies = {(j, k, h): query_copy(j, k, h) for j, k in others for h in range(HALVES)}
    for h in range(HALVES):
        q_copies[1, 0, h].start()
    for h in range(HALVES):
        for k in range(1, line):
            q_copies[0, k, h].start()

    def latent(i):
        return pl.ds(i * piece, piece)

    w_copies = [
        remote(pct.at[:, latent(i)], wholes[i], w_send.at[i], w_recv.at[i], on_group(2))
        for i in range(PIECES)
    ]
    for copy in w_copies:
        copy.start()

    def places_of(group):
        offs = [roff[i, group] for i in range(prompts)]
        lens = [plen[i, group] - lane * part for i in range(prompts)]
        ranks = []
        for i in range(prompts):
            rank = jnp.int32(0)
            for i2 in range(i):
                rank = rank + jnp.where(offs[i2] == offs[i], 1, 0)
            ranks.append(rank)

        def pick(distance, place):
            index, length, filled = jnp.int32(0), jnp.int32(0), jnp.int32(0)
            for i in range(prompts):
                hit = jnp.logical_and(offs[i] == distance, ranks[i] == place)
                index = jnp.where(hit, i, index)
                length = jnp.where(hit, lens[i], length)
                filled = jnp.where(hit, 1, filled)
            return index, length, filled

        return lens, [[pick(d, r) for r in range(CAPACITY)] for d in range(REACH)]

    for copy in loads[5:]:
        copy.wait()
    lens, slots = places_of(me)
    _, passing = places_of(lax.rem(me + groups - 2, groups))

    spots = lax.broadcasted_iota(jnp.int32, (piece, part), 1)

    def masked(ref, rows, slot):
        index, length, _ = slot
        block = ref[index, rows, :]
        return jnp.where(spots < length, block, jnp.zeros_like(block))

    n_copies = [
        remote(
            near.at[:, latent(i)], ac.at[pl.ds(0, CAPACITY), latent(i)],
            n_send.at[i], n_recv.at[i], on_group(1 - 2 * core),
        )
        for i in range(PIECES)
    ]
    loads[0].wait()

    @pl.when(core == 0)
    def _():
        for i in range(PIECES):
            for r in range(CAPACITY):
                near[r, latent(i), :] = masked(pctv, latent(i), slots[0][r])
            n_copies[i].start()

    far_slots = pl.ds((REACH - 1) * CAPACITY, CAPACITY)
    v_copies = [
        remote(
            given.at[:, latent(i)], via.at[:, latent(i)],
            v_send.at[i], v_recv.at[i], on_group(mid + 4),
        )
        for i in range(PIECES)
    ]
    b_copies = [
        remote(
            via.at[:, latent(i)], ac.at[far_slots, latent(i)],
            b_send.at[i], p_recv.at[i, REACH - 1], on_group(-mid),
        )
        for i in range(PIECES)
    ]

    @pl.when(giver)
    def _():
        for i in range(PIECES):
            for r in range(CAPACITY):
                given[r, latent(i), :] = masked(pctv, latent(i), slots[REACH - 1][r])
            v_copies[i].start()

    p_copies, keeps = [], []
    for i in range(PIECES):
        for d in range(1, REACH):
            src, dst = picked.at[d - 1, :, latent(i)], ac.at[pl.ds(d * CAPACITY, CAPACITY), latent(i)]
            if d == 1:
                keeps.append(pltpu.make_async_copy(src, dst, keep_sem.at[i]))
            else:
                p_copies.append(remote(src, dst, p_send.at[i, d], p_recv.at[i, d], on_group(d - 1)))

    def pass_on(i):
        w_copies[i].wait_recv()
        for d in range(REACH - 1, 0, -1):
            for r in range(CAPACITY):
                picked[d - 1, r, latent(i), :] = masked(wholes[i], slice(None), passing[d][r])
            if d == 1:
                keeps[i].start()
            else:
                copy = p_copies[i * (REACH - 2) + d - 2]
                if d == REACH - 1:
                    pl.when(jnp.logical_not(spared))(copy.start)
                else:
                    copy.start()

        @pl.when(core == 1)
        def _():
            for r in range(CAPACITY):
                near[r, latent(i), :] = masked(wholes[i], slice(None), passing[0][r])
            n_copies[i].start()

    def pass_when(*pieces, where):
        for i in pieces:
            pl.when(where)(functools.partial(pass_on, i))

    loads[4].wait()
    newkf[...] = jnp.zeros_like(newkf)
    for u in range(steps):
        step_rows = slv[u].astype(jnp.float32)
        for s in range(seqs):
            newkf[pl.ds(s * NEW_ROWS + u, 1), :] = step_rows[s:s + 1, :]
    newk[...] = newkf[...].astype(jnp.bfloat16)
    loads[2].wait()
    loads[3].wait()

    def resident(s):
        count = steps * heads
        query = rqv[:, s].reshape(count, width)
        fresh = newk.shape[0]
        old = matmul(query, rctv[s], NN) * SCALE
        new = matmul(query, newk[...], NT) * SCALE
        old_live = lax.broadcasted_iota(jnp.int32, (count, res_len), 1) < rlen[0, s]
        step = lax.broadcasted_iota(jnp.int32, (count, fresh), 0) // heads
        token = lax.broadcasted_iota(jnp.int32, (count, fresh), 1) - s * NEW_ROWS
        new_live = jnp.logical_and(token >= 0, token <= step)
        old = jnp.where(old_live, old, LOW)
        new = jnp.where(new_live, new, LOW)
        top = jnp.maximum(jnp.max(old, 1, keepdims=True), jnp.max(new, 1, keepdims=True))
        old = jnp.where(old_live, jnp.exp(old - top), 0.0)
        new = jnp.where(new_live, jnp.exp(new - top), 0.0)
        total = jnp.sum(old, 1, keepdims=True) + jnp.sum(new, 1, keepdims=True)
        mixed = matmul(old.astype(jnp.bfloat16), rctv[s, :LATENT_RANK, :], NT)
        mixed = mixed + matmul(new.astype(jnp.bfloat16), newk[:, :LATENT_RANK], NN)
        rov[:, s] = (mixed / total).astype(jnp.bfloat16).reshape(steps, heads, LATENT_RANK)

    for h in range(HALVES):
        q_copies[1, 0, h].wait_recv()
        for k in range(1, line):
            q_copies[1, k, h].start()

    for s in range(seqs // 2):
        resident(s)

    side = line * heads
    column = lax.broadcasted_iota(jnp.int32, (side, 128), 1)
    position = lax.broadcasted_iota(jnp.int32, (side, part), 1)
    o_copies = {0: [], 1: []}

    def send_back(copies):
        for copy in copies:
            copy.start()
        return copies

    def attend(j, chosen, stats):
        for p in chosen:
            query = qall[pl.ds(j * line, line), p].reshape(side, width)
            live = position < lens[p]
            scores = jnp.where(live, matmul(query, pctv[p], NN) * SCALE, LOW)
            top = jnp.max(scores, 1, keepdims=True)
            weights = jnp.where(live, jnp.exp(scores - top), 0.0)
            total = jnp.sum(weights, 1, keepdims=True)
            mixed = matmul(weights.astype(jnp.bfloat16), pctv[p, :LATENT_RANK, :], NT)
            obuf[pl.ds(j * line, line), p] = mixed.astype(jnp.bfloat16).reshape(line, heads, LATENT_RANK)
            stats = jnp.where(column == 2 * p, top, stats)
            stats = jnp.where(column == 2 * p + 1, total, stats)
        held, h = pl.ds(chosen[0], len(chosen)), chosen[0] // half
        o_copies[j] += send_back([
            remote(
                obuf.at[slot, held], rbuf.at[slot, held], o_send.at[slot, h], o_recv.at[slot, h],
                on_lane(0, (j + 1) * line - slot),
            )
            for slot in range(j * line + 1, (j + 1) * line)
        ])
        return stats

    def send_stats(j, stats):
        stat[pl.ds(j * line, line)] = stats.reshape(line, heads, 128)
        o_copies[j] += send_back([
            remote(
                stat.at[slot], rstat.at[slot], s_send.at[slot], s_recv.at[slot],
                on_lane(0, (j + 1) * line - slot),
            )
            for slot in range(j * line + 1, (j + 1) * line)
        ])

    def merged(p, parts):
        tops = [where[:, 2 * p:2 * p + 1] for where, _ in parts]
        sums = [where[:, 2 * p + 1:2 * p + 2] for where, _ in parts]
        top = functools.reduce(jnp.maximum, tops)
        total = jnp.zeros_like(top)
        mixed = jnp.zeros((heads, LATENT_RANK), jnp.float32)
        for own_top, own_sum, (_, values) in zip(tops, sums, parts):
            factor = jnp.exp(own_top - top)
            total = total + factor * own_sum
            mixed = mixed + factor * values[p].astype(jnp.float32)
        return top, total, mixed

    def parts_of(j):
        slots_of = [j * line + k for k in range(line)]
        return [
            ((stat if k == 0 else rstat).at[slot], (obuf if k == 0 else rbuf).at[slot])
            for k, slot in enumerate(slots_of)
        ]

    rest = jnp.logical_not(first)
    pass_when(0, where=rest)
    loads[1].wait()
    blank = jnp.zeros((side, 128), jnp.float32)
    for k in range(1, line):
        for h in range(HALVES):
            q_copies[0, k, h].wait_recv()
    send_stats(0, attend(0, range(prompts), blank))
    stats = blank
    for h in range(HALVES):
        for k in range(1, line):
            q_copies[1, k, h].wait_recv()
        stats = attend(1, range(h * half, (h + 1) * half), stats)
    send_stats(1, stats)

    @pl.when(bearer)
    def _():
        for there, on in zip(v_copies, b_copies):
            there.wait_recv()
            on.start()

    pass_when(1, 2, where=rest)
    for copy in o_copies[1]:
        copy.wait_recv()
    crossing = jnp.zeros((heads, 128), jnp.float32)
    lanes_of = lax.broadcasted_iota(jnp.int32, (heads, 128), 1)
    for p in range(prompts):
        top, total, mixed = merged(p, parts_of(1))
        xbuf[p] = mixed.astype(jnp.bfloat16)
        crossing = jnp.where(lanes_of == 2 * p, top, crossing)
        crossing = jnp.where(lanes_of == 2 * p + 1, total, crossing)
    xstat[...] = crossing
    crossings = ((xbuf, xrec, hop), (xstat, xrstat, hopstat))
    x_copies, out_copies, back_copies = [], [], []
    for i, (src, dst, via) in enumerate(crossings):
        x_copies.append(remote(src, dst, x_send.at[i], x_recv.at[i], on_lane(1, 0)))
        out_copies.append(remote(src, via, x_send.at[i], h_recv.at[i], beside(2)))
        back_copies.append(remote(via, dst, h_send.at[i], x_recv.at[i], on_group(-2)))

    @pl.when(first)
    def _():
        for copy in out_copies:
            copy.start()

    @pl.when(jnp.logical_not(first))
    def _():
        for copy in x_copies:
            copy.start()

    for s in range(seqs // 2, seqs):
        resident(s)
    pass_when(*range(PIECES), where=first)
    done = pltpu.make_async_copy(rov, ro, out_sem)
    done.start()

    for copy in o_copies[0]:
        copy.wait_recv()
    kept = jnp.zeros((heads, 128), jnp.float32)
    for p in range(prompts):
        top, total, mixed = merged(p, parts_of(0))
        mbuf[p] = mixed
        kept = jnp.where(lanes_of == 2 * p, top, kept)
        kept = jnp.where(lanes_of == 2 * p + 1, total, kept)
    mstat[...] = kept
    for copy in x_copies:
        copy.wait_recv()
    for p in range(prompts):
        _, total, mixed = merged(p, [(mstat, mbuf), (xrstat, xrec)])
        frows[p] = (mixed / jnp.maximum(total, 1.0)).astype(jnp.bfloat16)

    spread = lax.broadcasted_iota(jnp.int32, (heads, LATENT_RANK), 0)
    f_copies = []
    for d in range(REACH - 1, -1, -1):
        for r in range(CAPACITY):
            index, _, filled = slots[d][r]
            block = frows[index]
            fsend[d, r] = jnp.where(spread < filled * heads, block, jnp.zeros_like(block))
        copy = remote(
            fsend.at[d], fo.at[pl.ds(d * CAPACITY, CAPACITY)], f_send.at[d], f_recv.at[d], on_group(d + 1)
        )
        copy.start()
        f_copies.append(copy)

    @pl.when(second)
    def _():
        for out, back in zip(out_copies, back_copies):
            out.wait_recv()
            back.start()

    pass_when(3, where=rest)

    @pl.when(second)
    def _():
        for back in back_copies:
            back.wait_send()

    for copy in [done] + keeps:
        copy.wait()
    for copies in (q_copies.values(), o_copies[0], o_copies[1], x_copies, w_copies):
        for copy in copies:
            copy.wait_send()
    for copies in (n_copies, p_copies, f_copies):
        for copy in copies:
            copy.wait_recv()
    for copy in n_copies + f_copies:
        copy.wait_send()
    for i, copy in enumerate(p_copies):
        if i % (REACH - 2) == REACH - 3:
            pl.when(jnp.logical_not(spared))(copy.wait_send)
        else:
            copy.wait_send()
    for i in range(PIECES):
        pl.when(giver)(v_copies[i].wait_send)
        pl.when(bearer)(b_copies[i].wait_send)


def call(mesh_shape, plen, roff, rlen, sl, rct, rq, pct, pq):
    groups, lanes = mesh_shape
    prompts, width, part = pct.shape
    steps, seqs, heads, _ = rq.shape
    slots = REACH * CAPACITY
    bf, f32 = jnp.bfloat16, jnp.float32
    dma = pltpu.SemaphoreType.DMA
    anywhere = pl.BlockSpec(memory_space=pltpu.HBM)
    plen, roff, rlen, sl, rct, rq, pct, pq = [
        pltpu.with_memory_space_constraint(x, pltpu.HBM) for x in (plen, roff, rlen, sl, rct, rq, pct, pq)
    ]
    return pl.pallas_call(
        functools.partial(kernel, groups, lanes),
        out_shape=(
            jax.ShapeDtypeStruct((steps, seqs, heads, LATENT_RANK), bf),
            jax.ShapeDtypeStruct((slots, heads, LATENT_RANK), bf),
            jax.ShapeDtypeStruct((slots, width, part), bf),
        ),
        in_specs=[anywhere] * 8,
        out_specs=(pl.BlockSpec(memory_space=pl.ANY),) * 3,
        scratch_shapes=[
            pltpu.SMEM(plen.shape, jnp.int32),
            pltpu.SMEM(roff.shape, jnp.int32),
            pltpu.SMEM(rlen.shape, jnp.int32),
            pltpu.VMEM(rct.shape, bf),
            pltpu.VMEM(rq.shape, bf),
            pltpu.VMEM(pct.shape, bf),
            pltpu.VMEM(sl.shape, bf),
            pltpu.VMEM((lanes,) + pq.shape, bf),
            pltpu.VMEM((128, width), bf),
            pltpu.VMEM((128, width), f32),
            pltpu.VMEM((lanes, prompts, heads, LATENT_RANK), bf),
            pltpu.VMEM((lanes, prompts, heads, LATENT_RANK), bf),
            pltpu.VMEM((lanes, heads, 128), f32),
            pltpu.VMEM((lanes, heads, 128), f32),
            pltpu.VMEM((prompts, heads, LATENT_RANK), bf),
            pltpu.VMEM((prompts, heads, LATENT_RANK), bf),
            pltpu.VMEM((heads, 128), f32),
            pltpu.VMEM((heads, 128), f32),
            pltpu.VMEM((prompts, heads, LATENT_RANK), f32),
            pltpu.VMEM((heads, 128), f32),
            pltpu.VMEM((prompts, heads, LATENT_RANK), bf),
            pltpu.VMEM((heads, 128), f32),
            pltpu.VMEM((CAPACITY, width, part), bf),
            pltpu.VMEM((CAPACITY, width, part), bf),
            pltpu.VMEM((CAPACITY, width, part), bf),
            pltpu.VMEM((REACH - 1, CAPACITY, width, part), bf),
            pltpu.VMEM((prompts, heads, LATENT_RANK), bf),
            pltpu.VMEM((REACH, CAPACITY, heads, LATENT_RANK), bf),
            pltpu.VMEM((steps, seqs, heads, LATENT_RANK), bf),
            dma((8,)),
            dma,
            dma((lanes, HALVES)), dma((lanes, HALVES)),
            dma((lanes, HALVES)), dma((lanes, HALVES)),
            dma((lanes,)), dma((lanes,)),
            dma((2,)), dma((2,)),
            dma((2,)), dma((2,)),
            dma((PIECES,)), dma((PIECES,)),
            dma((PIECES,)), dma((PIECES,)),
            dma((PIECES, REACH)), dma((PIECES, REACH)),
            dma((PIECES,)),
            dma((REACH,)), dma((REACH,)),
            dma((PIECES,)), dma((PIECES,)), dma((PIECES,)),
        ] + [pltpu.VMEM((prompts, width // PIECES, part), bf)] * PIECES,
        compiler_params=pltpu.CompilerParams(
            collective_id=0, has_side_effects=True, vmem_limit_bytes=40 * 1024 * 1024
        ),
        name="decode_and_migrate",
    )(plen, roff, rlen, sl, rct, rq, pct, pq)


def writer(*refs):
    count = len(refs) // 2
    sems = refs[-1]
    copies = [pltpu.make_async_copy(refs[i], refs[count + i], sems.at[i]) for i in range(count)]
    for copy in copies:
        copy.start()
    for copy in copies:
        copy.wait()


def write_out(*arrays):
    arrays = [pltpu.with_memory_space_constraint(x, pltpu.VMEM) for x in arrays]
    return pl.pallas_call(
        writer,
        out_shape=tuple(jax.ShapeDtypeStruct(x.shape, x.dtype) for x in arrays),
        in_specs=[pl.BlockSpec(memory_space=pltpu.VMEM)] * len(arrays),
        out_specs=(pl.BlockSpec(memory_space=pltpu.HBM),) * len(arrays),
        scratch_shapes=[pltpu.SemaphoreType.DMA((len(arrays),))],
        name="write_out",
    )(*arrays)


def solution(mesh):
    mesh_shape = (mesh.shape["grp"], mesh.shape["head"])

    def body(
        resident_latent_cache, resident_len, resident_query, step_latent,
        prompt_cache, prompt_query, prompt_len, route_offset,
    ):
        ro, fo, ac = write_out(*call(
            mesh_shape,
            prompt_len.T,
            route_offset[:, :, 0].T,
            resident_len,
            step_latent,
            jnp.swapaxes(resident_latent_cache, 1, 2),
            resident_query,
            jnp.swapaxes(prompt_cache, 1, 2),
            prompt_query,
        ))
        return ro, fo[None], jnp.swapaxes(ac, 1, 2)[None]

    in_specs = (
        P("grp", None, None),
        P("grp", None),
        P(None, "grp", "head", None),
        P(None, "grp", None),
        P("grp", "head", None),
        P("grp", "head", None),
        P(),
        P(),
    )
    out_specs = (
        P(None, "grp", "head", None),
        P("grp", None, "head", None),
        P("grp", None, "head", None),
    )
    return jax.shard_map(body, mesh=mesh, in_specs=in_specs, out_specs=out_specs, check_vma=False)
```

```python
import functools

import jax
import jax.numpy as jnp
from jax import lax
from jax.experimental import pallas as pl
from jax.experimental.pallas import tpu as pltpu
from jax.sharding import PartitionSpec as P

LATENT_RANK = 512
REACH = 4
CAPACITY = 2
MESH = pl.DeviceIdType.MESH
SCALE = 192.0 ** (-0.5)
LOW = -1e30
NEW_ROWS = 16

FAR = 2
HALVES = 2
PIECES = 4

NN = (((1,), (0,)), ((), ()))
NT = (((1,), (1,)), ((), ()))


def matmul(a, b, dims):
    return lax.dot_general(a, b, dims, preferred_element_type=jnp.float32)


def kernel(
    groups, lanes,
    plen_hbm, roff_hbm, rlen_hbm, sl, rct, rq, pct, pq,
    ro, fo, ac,
    plen, roff, rlen,
    rctv, rqv, pctv, slv, pqv, qall, ktail, newk, newkf, obuf, rbuf, stat, rstat, xbuf, xrec, xstat, xrstat, mbuf, mstat, hop, hopstat, given, via, near, picked, frows, fsend, rov,
    load_sem, out_sem, q_send, q_recv, o_send, o_recv, s_send, s_recv, x_send, x_recv, h_send, h_recv,
    w_send, w_recv, n_send, n_recv, p_send, p_recv, keep_sem, f_send, f_recv, v_send, v_recv, b_send,
    *wholes,
):
    me = lax.axis_index("grp")
    lane = lax.axis_index("head")
    core = lax.rem(me, 2)
    prompts, width, part = pct.shape
    seqs = rct.shape[0]
    res_len = rct.shape[2]
    steps, _, heads, _ = rq.shape
    line = lanes // FAR
    piece = width // PIECES

    y, x = lane // FAR, lax.rem(lane, FAR)

    def on_lane(j, k):
        return (me, lax.rem(y + k, line) * FAR + lax.rem(x + j, FAR))

    def on_group(k):
        return (lax.rem(me + k + groups, groups), lane)

    direct = [(1, 0)] + [(0, k) for k in range(1, line)]
    others = direct + [(1, k) for k in range(1, line)]
    turn = lax.rem(me, groups // 2)
    first = turn < 2
    second = jnp.logical_and(turn >= 2, turn < 4)
    mid = (groups // 2 - 4) // 4 * 2
    giver, bearer, taker = turn == groups // 2 - 4, turn == mid, turn == 0
    spared = turn == groups // 2 - 2

    barrier = pltpu.get_barrier_semaphore()

    def greet(to):
        pl.semaphore_signal(barrier, inc=1, device_id=to, device_id_type=MESH)

    def beside(k):
        return (on_group(k)[0], on_lane(1, 0)[1])

    for k in range(REACH, 0, -1):
        greet(on_group(-k))
    for j, k in direct:
        greet(on_lane(j, k))
    pl.when(core == 0)(lambda: greet(on_group(1)))
    pl.when(taker)(lambda: greet(on_group(mid)))
    pl.when(bearer)(lambda: greet(on_group(-mid - 4)))
    pl.when(first)(lambda: greet(on_group(2)))
    pl.when(second)(lambda: greet(beside(-2)))

    loads = [
        pltpu.make_async_copy(src, dst, load_sem.at[i])
        for i, (src, dst) in enumerate(((pct, pctv), (pq, pqv), (rct, rctv), (rq, rqv), (sl, slv),
                                    (plen_hbm, plen), (roff_hbm, roff), (rlen_hbm, rlen)))
    ]
    for copy in loads:
        copy.start()

    half = prompts // HALVES
    tail = width - LATENT_RANK
    loads[1].wait()
    for h in range(HALVES):
        for i in range(half):
            qall[0, h, :, pl.ds(i * LATENT_RANK, LATENT_RANK)] = pqv[h * half + i, :, :LATENT_RANK]
        tails = [pqv[h * half + i, :, LATENT_RANK:] for i in range(half)]
        qall[0, h, :, pl.ds(half * LATENT_RANK, half * tail)] = jnp.concatenate(tails, axis=1)

    extra = core + jnp.where(jnp.logical_or(first, second), 1, 0)
    extra = extra + jnp.where(jnp.logical_or(giver, bearer), 1, 0)
    pl.semaphore_wait(barrier, len(direct) + REACH + extra)

    def remote(src, dst, send, recv, to):
        return pltpu.make_async_remote_copy(
            src_ref=src, dst_ref=dst, send_sem=send, recv_sem=recv, device_id=to, device_id_type=MESH
        )

    def query_copy(j, k, h):
        slot, source = j * line + k, qall.at[j * line if j and k else 0, h]
        return remote(source, qall.at[slot, h], q_send.at[slot, h], q_recv.at[slot, h], on_lane(0 if k else j, k))

    q_copies = {(j, k, h): query_copy(j, k, h) for j, k in others for h in range(HALVES)}
    for h in range(HALVES):
        q_copies[1, 0, h].start()
    for h in range(HALVES):
        for k in range(1, line):
            q_copies[0, k, h].start()

    def latent(i):
        return pl.ds(i * piece, piece)

    w_copies = [
        remote(pct.at[:, latent(i)], wholes[i], w_send.at[i], w_recv.at[i], on_group(2))
        for i in range(PIECES)
    ]
    for copy in w_copies:
        copy.start()

    def places_of(group):
        offs = [roff[i, group] for i in range(prompts)]
        lens = [plen[i, group] - lane * part for i in range(prompts)]
        ranks = []
        for i in range(prompts):
            rank = jnp.int32(0)
            for i2 in range(i):
                rank = rank + jnp.where(offs[i2] == offs[i], 1, 0)
            ranks.append(rank)

        def pick(distance, place):
            index, length, filled = jnp.int32(0), jnp.int32(0), jnp.int32(0)
            for i in range(prompts):
                hit = jnp.logical_and(offs[i] == distance, ranks[i] == place)
                index = jnp.where(hit, i, index)
                length = jnp.where(hit, lens[i], length)
                filled = jnp.where(hit, 1, filled)
            return index, length, filled

        return lens, [[pick(d, r) for r in range(CAPACITY)] for d in range(REACH)]

    for copy in loads[5:]:
        copy.wait()
    lens, slots = places_of(me)
    _, passing = places_of(lax.rem(me + groups - 2, groups))

    spots = lax.broadcasted_iota(jnp.int32, (piece, part), 1)

    def masked(ref, rows, slot):
        index, length, _ = slot
        block = ref[index, rows, :]
        return jnp.where(spots < length, block, jnp.zeros_like(block))

    n_copies = [
        remote(
            near.at[:, latent(i)], ac.at[pl.ds(0, CAPACITY), latent(i)],
            n_send.at[i], n_recv.at[i], on_group(1 - 2 * core),
        )
        for i in range(PIECES)
    ]
    loads[0].wait()

    @pl.when(core == 0)
    def _():
        for i in range(PIECES):
            for r in range(CAPACITY):
                near[r, latent(i), :] = masked(pctv, latent(i), slots[0][r])
            n_copies[i].start()

    far_slots = pl.ds((REACH - 1) * CAPACITY, CAPACITY)
    v_copies = [
        remote(
            given.at[:, latent(i)], via.at[:, latent(i)],
            v_send.at[i], v_recv.at[i], on_group(mid + 4),
        )
        for i in range(PIECES)
    ]
    b_copies = [
        remote(
            via.at[:, latent(i)], ac.at[far_slots, latent(i)],
            b_send.at[i], p_recv.at[i, REACH - 1], on_group(-mid),
        )
        for i in range(PIECES)
    ]

    @pl.when(giver)
    def _():
        for i in range(PIECES):
            for r in range(CAPACITY):
                given[r, latent(i), :] = masked(pctv, latent(i), slots[REACH - 1][r])
            v_copies[i].start()

    p_copies, keeps = [], []
    for i in range(PIECES):
        for d in range(1, REACH):
            src, dst = picked.at[d - 1, :, latent(i)], ac.at[pl.ds(d * CAPACITY, CAPACITY), latent(i)]
            if d == 1:
                keeps.append(pltpu.make_async_copy(src, dst, keep_sem.at[i]))
            else:
                p_copies.append(remote(src, dst, p_send.at[i, d], p_recv.at[i, d], on_group(d - 1)))

    def pass_on(i):
        w_copies[i].wait_recv()
        for d in range(REACH - 1, 0, -1):
            for r in range(CAPACITY):
                picked[d - 1, r, latent(i), :] = masked(wholes[i], slice(None), passing[d][r])
            if d == 1:
                keeps[i].start()
            else:
                copy = p_copies[i * (REACH - 2) + d - 2]
                if d == REACH - 1:
                    pl.when(jnp.logical_not(spared))(copy.start)
                else:
                    copy.start()

        @pl.when(core == 1)
        def _():
            for r in range(CAPACITY):
                near[r, latent(i), :] = masked(wholes[i], slice(None), passing[0][r])
            n_copies[i].start()

    def pass_when(*pieces, where):
        for i in pieces:
            pl.when(where)(functools.partial(pass_on, i))

    ktail[...] = jnp.zeros_like(ktail)
    for p in range(prompts):
        ktail[p, pl.ds(p % half * tail, tail), :] = pctv[p, LATENT_RANK:, :]

    loads[4].wait()
    newkf[...] = jnp.zeros_like(newkf)
    for u in range(steps):
        step_rows = slv[u].astype(jnp.float32)
        for s in range(seqs):
            newkf[pl.ds(s * NEW_ROWS + u, 1), :] = step_rows[s:s + 1, :]
    newk[...] = newkf[...].astype(jnp.bfloat16)
    loads[2].wait()
    loads[3].wait()

    def resident(s):
        count = steps * heads
        query = rqv[:, s].reshape(count, width)
        fresh = newk.shape[0]
        old = matmul(query, rctv[s], NN) * SCALE
        new = matmul(query, newk[...], NT) * SCALE
        old_live = lax.broadcasted_iota(jnp.int32, (count, res_len), 1) < rlen[0, s]
        step = lax.broadcasted_iota(jnp.int32, (count, fresh), 0) // heads
        token = lax.broadcasted_iota(jnp.int32, (count, fresh), 1) - s * NEW_ROWS
        new_live = jnp.logical_and(token >= 0, token <= step)
        old = jnp.where(old_live, old, LOW)
        new = jnp.where(new_live, new, LOW)
        top = jnp.maximum(jnp.max(old, 1, keepdims=True), jnp.max(new, 1, keepdims=True))
        old = jnp.where(old_live, jnp.exp(old - top), 0.0)
        new = jnp.where(new_live, jnp.exp(new - top), 0.0)
        total = jnp.sum(old, 1, keepdims=True) + jnp.sum(new, 1, keepdims=True)
        mixed = matmul(old.astype(jnp.bfloat16), rctv[s, :LATENT_RANK, :], NT)
        mixed = mixed + matmul(new.astype(jnp.bfloat16), newk[:, :LATENT_RANK], NN)
        rov[:, s] = (mixed / total).astype(jnp.bfloat16).reshape(steps, heads, LATENT_RANK)

    for h in range(HALVES):
        q_copies[1, 0, h].wait_recv()
        for k in range(1, line):
            q_copies[1, k, h].start()

    for s in range(seqs // 2):
        resident(s)

    side = line * heads
    column = lax.broadcasted_iota(jnp.int32, (side, 128), 1)
    position = lax.broadcasted_iota(jnp.int32, (side, part), 1)
    o_copies = {0: [], 1: []}

    def send_back(copies):
        for copy in copies:
            copy.start()
        return copies

    def attend(j, chosen, stats):
        for p in chosen:
            h, place = p // half, p % half
            query = qall[pl.ds(j * line, line), h, :, pl.ds(place * LATENT_RANK, LATENT_RANK)]
            rest_of = qall[pl.ds(j * line, line), h, :, pl.ds(half * LATENT_RANK, half * tail)]
            scores = matmul(query.reshape(side, LATENT_RANK), pctv[p, :LATENT_RANK, :], NN)
            scores = scores + matmul(rest_of.reshape(side, half * tail), ktail[p], NN)
            live = position < lens[p]
            scores = jnp.where(live, scores * SCALE, LOW)
            top = jnp.max(scores, 1, keepdims=True)
            weights = jnp.where(live, jnp.exp(scores - top), 0.0)
            total = jnp.sum(weights, 1, keepdims=True)
            mixed = matmul(weights.astype(jnp.bfloat16), pctv[p, :LATENT_RANK, :], NT)
            obuf[pl.ds(j * line, line), p] = mixed.astype(jnp.bfloat16).reshape(line, heads, LATENT_RANK)
            stats = jnp.where(column == 2 * p, top, stats)
            stats = jnp.where(column == 2 * p + 1, total, stats)
        held, h = pl.ds(chosen[0], len(chosen)), chosen[0] // half
        o_copies[j] += send_back([
            remote(
                obuf.at[slot, held], rbuf.at[slot, held], o_send.at[slot, h], o_recv.at[slot, h],
                on_lane(0, (j + 1) * line - slot),
            )
            for slot in range(j * line + 1, (j + 1) * line)
        ])
        return stats

    def send_stats(j, stats):
        stat[pl.ds(j * line, line)] = stats.reshape(line, heads, 128)
        o_copies[j] += send_back([
            remote(
                stat.at[slot], rstat.at[slot], s_send.at[slot], s_recv.at[slot],
                on_lane(0, (j + 1) * line - slot),
            )
            for slot in range(j * line + 1, (j + 1) * line)
        ])

    def merged(p, parts):
        tops = [where[:, 2 * p:2 * p + 1] for where, _ in parts]
        sums = [where[:, 2 * p + 1:2 * p + 2] for where, _ in parts]
        top = functools.reduce(jnp.maximum, tops)
        total = jnp.zeros_like(top)
        mixed = jnp.zeros((heads, LATENT_RANK), jnp.float32)
        for own_top, own_sum, (_, values) in zip(tops, sums, parts):
            factor = jnp.exp(own_top - top)
            total = total + factor * own_sum
            mixed = mixed + factor * values[p].astype(jnp.float32)
        return top, total, mixed

    def parts_of(j):
        slots_of = [j * line + k for k in range(line)]
        return [
            ((stat if k == 0 else rstat).at[slot], (obuf if k == 0 else rbuf).at[slot])
            for k, slot in enumerate(slots_of)
        ]

    rest = jnp.logical_not(first)
    pass_when(0, where=rest)
    blank = jnp.zeros((side, 128), jnp.float32)
    for k in range(1, line):
        for h in range(HALVES):
            q_copies[0, k, h].wait_recv()
    send_stats(0, attend(0, range(prompts), blank))
    stats = blank
    for h in range(HALVES):
        for k in range(1, line):
            q_copies[1, k, h].wait_recv()
        stats = attend(1, range(h * half, (h + 1) * half), stats)
    send_stats(1, stats)

    @pl.when(bearer)
    def _():
        for there, on in zip(v_copies, b_copies):
            there.wait_recv()
            on.start()

    pass_when(1, 2, where=rest)
    for copy in o_copies[1]:
        copy.wait_recv()
    crossing = jnp.zeros((heads, 128), jnp.float32)
    lanes_of = lax.broadcasted_iota(jnp.int32, (heads, 128), 1)
    for p in range(prompts):
        top, total, mixed = merged(p, parts_of(1))
        xbuf[p] = mixed.astype(jnp.bfloat16)
        crossing = jnp.where(lanes_of == 2 * p, top, crossing)
        crossing = jnp.where(lanes_of == 2 * p + 1, total, crossing)
    xstat[...] = crossing
    crossings = ((xbuf, xrec, hop), (xstat, xrstat, hopstat))
    x_copies, out_copies, back_copies = [], [], []
    for i, (src, dst, via) in enumerate(crossings):
        x_copies.append(remote(src, dst, x_send.at[i], x_recv.at[i], on_lane(1, 0)))
        out_copies.append(remote(src, via, x_send.at[i], h_recv.at[i], beside(2)))
        back_copies.append(remote(via, dst, h_send.at[i], x_recv.at[i], on_group(-2)))

    @pl.when(first)
    def _():
        for copy in out_copies:
            copy.start()

    @pl.when(jnp.logical_not(first))
    def _():
        for copy in x_copies:
            copy.start()

    for s in range(seqs // 2, seqs):
        resident(s)
    pass_when(*range(PIECES), where=first)
    done = pltpu.make_async_copy(rov, ro, out_sem)
    done.start()

    for copy in o_copies[0]:
        copy.wait_recv()
    kept = jnp.zeros((heads, 128), jnp.float32)
    for p in range(prompts):
        top, total, mixed = merged(p, parts_of(0))
        mbuf[p] = mixed
        kept = jnp.where(lanes_of == 2 * p, top, kept)
        kept = jnp.where(lanes_of == 2 * p + 1, total, kept)
    mstat[...] = kept
    for copy in x_copies:
        copy.wait_recv()
    for p in range(prompts):
        _, total, mixed = merged(p, [(mstat, mbuf), (xrstat, xrec)])
        frows[p] = (mixed / jnp.maximum(total, 1.0)).astype(jnp.bfloat16)

    spread = lax.broadcasted_iota(jnp.int32, (heads, LATENT_RANK), 0)
    f_copies = []
    for d in range(REACH - 1, -1, -1):
        for r in range(CAPACITY):
            index, _, filled = slots[d][r]
            block = frows[index]
            fsend[d, r] = jnp.where(spread < filled * heads, block, jnp.zeros_like(block))
        copy = remote(
            fsend.at[d], fo.at[pl.ds(d * CAPACITY, CAPACITY)], f_send.at[d], f_recv.at[d], on_group(d + 1)
        )
        copy.start()
        f_copies.append(copy)

    @pl.when(second)
    def _():
        for out, back in zip(out_copies, back_copies):
            out.wait_recv()
            back.start()

    pass_when(3, where=rest)

    @pl.when(second)
    def _():
        for back in back_copies:
            back.wait_send()

    for copy in [done] + keeps:
        copy.wait()
    for copies in (q_copies.values(), o_copies[0], o_copies[1], x_copies, w_copies):
        for copy in copies:
            copy.wait_send()
    for copies in (n_copies, p_copies, f_copies):
        for copy in copies:
            copy.wait_recv()
    for copy in n_copies + f_copies:
        copy.wait_send()
    for i, copy in enumerate(p_copies):
        if i % (REACH - 2) == REACH - 3:
            pl.when(jnp.logical_not(spared))(copy.wait_send)
        else:
            copy.wait_send()
    for i in range(PIECES):
        pl.when(giver)(v_copies[i].wait_send)
        pl.when(bearer)(b_copies[i].wait_send)


def call(mesh_shape, plen, roff, rlen, sl, rct, rq, pct, pq):
    groups, lanes = mesh_shape
    prompts, width, part = pct.shape
    steps, seqs, heads, _ = rq.shape
    slots = REACH * CAPACITY
    bf, f32 = jnp.bfloat16, jnp.float32
    dma = pltpu.SemaphoreType.DMA
    anywhere = pl.BlockSpec(memory_space=pltpu.HBM)
    plen, roff, rlen, sl, rct, rq, pct, pq = [
        pltpu.with_memory_space_constraint(x, pltpu.HBM) for x in (plen, roff, rlen, sl, rct, rq, pct, pq)
    ]
    return pl.pallas_call(
        functools.partial(kernel, groups, lanes),
        out_shape=(
            jax.ShapeDtypeStruct((steps, seqs, heads, LATENT_RANK), bf),
            jax.ShapeDtypeStruct((slots, heads, LATENT_RANK), bf),
            jax.ShapeDtypeStruct((slots, width, part), bf),
        ),
        in_specs=[anywhere] * 8,
        out_specs=(pl.BlockSpec(memory_space=pl.ANY),) * 3,
        scratch_shapes=[
            pltpu.SMEM(plen.shape, jnp.int32),
            pltpu.SMEM(roff.shape, jnp.int32),
            pltpu.SMEM(rlen.shape, jnp.int32),
            pltpu.VMEM(rct.shape, bf),
            pltpu.VMEM(rq.shape, bf),
            pltpu.VMEM(pct.shape, bf),
            pltpu.VMEM(sl.shape, bf),
            pltpu.VMEM(pq.shape, bf),
            pltpu.VMEM((lanes, HALVES, heads, prompts // HALVES * width), bf),
            pltpu.VMEM((prompts, prompts // HALVES * (width - LATENT_RANK), part), bf),
            pltpu.VMEM((128, width), bf),
            pltpu.VMEM((128, width), f32),
            pltpu.VMEM((lanes, prompts, heads, LATENT_RANK), bf),
            pltpu.VMEM((lanes, prompts, heads, LATENT_RANK), bf),
            pltpu.VMEM((lanes, heads, 128), f32),
            pltpu.VMEM((lanes, heads, 128), f32),
            pltpu.VMEM((prompts, heads, LATENT_RANK), bf),
            pltpu.VMEM((prompts, heads, LATENT_RANK), bf),
            pltpu.VMEM((heads, 128), f32),
            pltpu.VMEM((heads, 128), f32),
            pltpu.VMEM((prompts, heads, LATENT_RANK), f32),
            pltpu.VMEM((heads, 128), f32),
            pltpu.VMEM((prompts, heads, LATENT_RANK), bf),
            pltpu.VMEM((heads, 128), f32),
            pltpu.VMEM((CAPACITY, width, part), bf),
            pltpu.VMEM((CAPACITY, width, part), bf),
            pltpu.VMEM((CAPACITY, width, part), bf),
            pltpu.VMEM((REACH - 1, CAPACITY, width, part), bf),
            pltpu.VMEM((prompts, heads, LATENT_RANK), bf),
            pltpu.VMEM((REACH, CAPACITY, heads, LATENT_RANK), bf),
            pltpu.VMEM((steps, seqs, heads, LATENT_RANK), bf),
            dma((8,)),
            dma,
            dma((lanes, HALVES)), dma((lanes, HALVES)),
            dma((lanes, HALVES)), dma((lanes, HALVES)),
            dma((lanes,)), dma((lanes,)),
            dma((2,)), dma((2,)),
            dma((2,)), dma((2,)),
            dma((PIECES,)), dma((PIECES,)),
            dma((PIECES,)), dma((PIECES,)),
            dma((PIECES, REACH)), dma((PIECES, REACH)),
            dma((PIECES,)),
            dma((REACH,)), dma((REACH,)),
            dma((PIECES,)), dma((PIECES,)), dma((PIECES,)),
        ] + [pltpu.VMEM((prompts, width // PIECES, part), bf)] * PIECES,
        compiler_params=pltpu.CompilerParams(
            collective_id=0, has_side_effects=True, vmem_limit_bytes=40 * 1024 * 1024
        ),
        name="decode_and_migrate",
    )(plen, roff, rlen, sl, rct, rq, pct, pq)


def writer(*refs):
    count = len(refs) // 2
    sems = refs[-1]
    copies = [pltpu.make_async_copy(refs[i], refs[count + i], sems.at[i]) for i in range(count)]
    for copy in copies:
        copy.start()
    for copy in copies:
        copy.wait()


def write_out(*arrays):
    arrays = [pltpu.with_memory_space_constraint(x, pltpu.VMEM) for x in arrays]
    return pl.pallas_call(
        writer,
        out_shape=tuple(jax.ShapeDtypeStruct(x.shape, x.dtype) for x in arrays),
        in_specs=[pl.BlockSpec(memory_space=pltpu.VMEM)] * len(arrays),
        out_specs=(pl.BlockSpec(memory_space=pltpu.HBM),) * len(arrays),
        scratch_shapes=[pltpu.SemaphoreType.DMA((len(arrays),))],
        name="write_out",
    )(*arrays)


def solution(mesh):
    mesh_shape = (mesh.shape["grp"], mesh.shape["head"])

    def body(
        resident_latent_cache, resident_len, resident_query, step_latent,
        prompt_cache, prompt_query, prompt_len, route_offset,
    ):
        ro, fo, ac = write_out(*call(
            mesh_shape,
            prompt_len.T,
            route_offset[:, :, 0].T,
            resident_len,
            step_latent,
            jnp.swapaxes(resident_latent_cache, 1, 2),
            resident_query,
            jnp.swapaxes(prompt_cache, 1, 2),
            prompt_query,
        ))
        return ro, fo[None], jnp.swapaxes(ac, 1, 2)[None]

    in_specs = (
        P("grp", None, None),
        P("grp", None),
        P(None, "grp", "head", None),
        P(None, "grp", None),
        P("grp", "head", None),
        P("grp", "head", None),
        P(),
        P(),
    )
    out_specs = (
        P(None, "grp", "head", None),
        P("grp", None, "head", None),
        P("grp", None, "head", None),
    )
    return jax.shard_map(body, mesh=mesh, in_specs=in_specs, out_specs=out_specs, check_vma=False)
```
